128 devices in a mesh: gx: 4 (over y), gy: 32 (over z, x, core).
Axes of the slice: x: 4, y: 4, z: 4, core: 2. Of those that a mesh axis runs over, the one named last changes fastest.
Arguments:
- rhs: float32 [32, 256, 128], P('gy', 'gx'), may hold values from -6 to 6
- fine_blocks: float32 [32, 256, 3, 128, 128], P('gy', 'gx'), may hold values from -1 to 5
- smoother: float32 [32, 256, 128, 128], P('gy', 'gx'), may hold values from -0.1 to 0.3
- columns: int32 [32, 256, 3], P('gy', 'gx'), may hold values from 0 to 255, as said below
- aggregates: int32 [32, 256, 128], P('gy', 'gx'), may hold values from 0 to 16383, as said below
- weights: float32 [32, 256, 128], P('gy', 'gx'), may hold values from 0.1 to 0.3
- coarse_lower: float32 [128, 128, 128], P('gy'), may hold values from -1.2 to 0.3
- coarse_upper: float32 [128, 128, 128], P('gy'), may hold values from -1.2 to 0.3
- coarse_pivot: float32 [128, 128, 128], P('gy'), may hold values from -0.3 to 1.7
Outputs:
- solution_field: float32 [32, 256, 128], P('gy', 'gx')
- coarse_solution: float32 [128, 128], P('gy')
The draws below stay inside these ranges and needn't reach their ends.
Inputs may be any that keep to these rules, and one draw needn't show every extreme that they name: `columns`: column 0 of each block row is the row itself; every other column lies within 2 blocks of the row in the same line. With g = (l * 256 + n) * 128 + b the fine row's index over all lines, aggregates[l, n, b] differs by at most 256 from g // 64; the first fine row takes 0 and the last 16383.
All inputs are finite; a program needn't handle non-finite values.
Results may differ from the reference program's by a relative error of at most 0.0003.
Values sent between devices are 32-bit elements; how exact they have to be, the bound alone decides.
No kernel may reach another device: no remote copies, remote signals or barrier semaphores. Data moves between devices by JAX's collectives and lax.ppermute only.
A program may use at most 128 MiB of HBM per device.

```python
import math
import jax
import jax.numpy as jnp
from jax import lax

BS = 128
K = 3
HB = 2
NCB = 128
SWEEPS = 2
LINES = 32
LBLK = 256


def unit_matrix(size):
    index = jnp.arange(size)
    return (index[:, None] == index[None, :]).astype(jnp.float32)


def draw_fine_blocks(key, part):
    key = jax.random.fold_in(key, 11)
    shape = (LINES, LBLK, K, BS, BS)
    noise = jax.random.normal(key, shape, jnp.float32)
    first = (jnp.arange(K) == 0).astype(jnp.float32)[:, None, None]
    return noise * (0.5 / math.sqrt(BS)) + 4.0 * first * unit_matrix(BS)


def draw_smoother(key, part):
    key = jax.random.fold_in(key, 12)
    shape = (LINES, LBLK, BS, BS)
    noise = jax.random.normal(key, shape, jnp.float32)
    return noise * (0.03 / math.sqrt(BS)) + 0.2 * unit_matrix(BS)


def draw_columns(key, part):
    key = jax.random.fold_in(key, 13)
    key_size, key_sign = jax.random.split(key)
    shape = (LINES, LBLK, K - 1)
    row = jnp.arange(LBLK, dtype=jnp.int32)[None, :, None]
    distance = jax.random.randint(key_size, shape, 1, HB + 1)
    offset = distance * (jax.random.randint(key_sign, shape, 0, 2) * 2 - 1)
    moved = row + offset
    moved = jnp.where((moved < 0) | (moved >= LBLK), row - offset, moved)
    first = jnp.broadcast_to(row, (LINES, LBLK, 1))
    return jnp.concatenate([first, moved], axis=2).astype(jnp.int32)


def draw_aggregates(key, part):
    key = jax.random.fold_in(key, 17)
    shape = (LINES, LBLK, BS)
    ratio = LINES * LBLK // NCB
    line_index = jnp.arange(LINES, dtype=jnp.int32)[:, None, None]
    block_index = jnp.arange(LBLK, dtype=jnp.int32)[None, :, None]
    row_index = jnp.arange(BS, dtype=jnp.int32)[None, None, :]
    global_row = (line_index * LBLK + block_index) * BS + row_index
    base = global_row // ratio
    jitter = jax.random.randint(key, shape, -2 * BS, 2 * BS + 1).astype(jnp.int32)
    last_row = LINES * LBLK * BS - 1
    jitter = jnp.where((global_row == 0) | (global_row == last_row), 0, jitter)
    return jnp.clip(base + jitter, 0, NCB * BS - 1).astype(jnp.int32)


def slow_channels(key, share):
    chooser = jax.random.uniform(jax.random.fold_in(key, 99), (BS,), jnp.float32)
    return (chooser < share).astype(jnp.float32)


def factor_blocks(key, noise, low, high, slow, slow_low, slow_high, sign, noise_scale):
    key_fast, key_slow = jax.random.split(key)
    fast_gain = jax.random.uniform(key_fast, (NCB, BS), jnp.float32, low, high)
    slow_gain = jax.random.uniform(key_slow, (NCB, BS), jnp.float32, slow_low, slow_high)
    gains = slow[None, :] * slow_gain + (1.0 - slow[None, :]) * fast_gain
    return sign * gains[:, :, None] * unit_matrix(BS) + noise * (noise_scale / math.sqrt(BS))


def coarse_noise(key):
    return jax.random.normal(key, (NCB, BS, BS), jnp.float32)


def slow_share():
    return 0.5


def draw_coarse_lower(key, part):
    slow = slow_channels(key, slow_share())
    key = jax.random.fold_in(key, 14)
    key_gain, key_noise = jax.random.split(key)
    return factor_blocks(key_gain, coarse_noise(key_noise), 0.2, 0.6, slow, 0.95, 0.985, -1.0, 0.04)


def draw_coarse_upper(key, part):
    slow = slow_channels(key, slow_share())
    key = jax.random.fold_in(key, 15)
    key_gain, key_noise = jax.random.split(key)
    return factor_blocks(key_gain, coarse_noise(key_noise), 0.2, 0.6, slow, 0.95, 0.985, -1.0, 0.04)


def draw_coarse_pivot(key, part):
    slow = slow_channels(key, slow_share())
    key = jax.random.fold_in(key, 16)
    key_gain, key_noise = jax.random.split(key)
    return factor_blocks(key_gain, coarse_noise(key_noise), 0.5, 1.5, slow, 0.9, 1.0, 1.0, 0.1)


def block_levels(own_key, extent, shards, low, largest):
    factor_of = 1.0
    for axis_at, parts in shards:
        heights = jax.random.uniform(jax.random.fold_in(jax.random.fold_in(own_key, 6), axis_at), (parts,), jnp.float32, low / len(shards), largest / len(shards))
        factor_of = factor_of * jnp.repeat(jnp.exp(heights), extent[axis_at] // parts).reshape((-1,) + (1,) * (len(extent) - 1 - axis_at))
    return factor_of


def bell_draw(key, dims, deviation, reach, cuts=(), kind=jnp.bfloat16):
    values = jax.random.normal(key, dims, jnp.float32) * deviation
    if len(cuts) > 0:
        values = block_levels(key, dims, cuts, -0.22, 0.18) * values
    return jnp.clip(values, min=-reach, max=reach).astype(kind)


def setup_inputs(seed: int = 0) -> dict:
    arg_keys = jax.random.split(jax.random.key(seed), 10)
    return {
        "rhs": bell_draw(arg_keys[0], (LINES, LBLK, BS), 1.0, 6.0, ((0, 32), (1, 4)), jnp.float32),
        "fine_blocks": draw_fine_blocks(jax.random.fold_in(arg_keys[9], 71), 0),
        "smoother": draw_smoother(jax.random.fold_in(arg_keys[9], 71), 0),
        "columns": draw_columns(jax.random.fold_in(arg_keys[9], 71), 0),
        "aggregates": draw_aggregates(jax.random.fold_in(arg_keys[9], 71), 0),
        "weights": jnp.clip(0.1 + 0.20000001043081284 * jax.random.uniform(arg_keys[5], (LINES, LBLK, BS), jnp.float32) ** block_levels(arg_keys[5], (LINES, LBLK, BS), ((0, 32), (1, 4)), -0.2, 0.2), 0.1, 0.3),
        "coarse_lower": draw_coarse_lower(jax.random.fold_in(arg_keys[9], 71), 0),
        "coarse_upper": draw_coarse_upper(jax.random.fold_in(arg_keys[9], 71), 0),
        "coarse_pivot": draw_coarse_pivot(jax.random.fold_in(arg_keys[9], 71), 0),
    }


highest = lax.Precision.HIGHEST


def apply_operator(fine_blocks, field, columns):
    picked = jax.vmap(lambda line_field, line_columns: line_field[line_columns])(field, columns)
    return jnp.einsum('lnkab,lnkb->lna', fine_blocks, picked, precision=highest)


def sweep_once(fine_blocks, smoother, columns, rhs, field):
    leftover = rhs - apply_operator(fine_blocks, field, columns)
    return field + jnp.einsum('lnab,lnb->lna', smoother, leftover, precision=highest)


def coarse_solve(coarse_lower, coarse_upper, coarse_pivot, coarse_rhs):
    zero_block = jnp.zeros((coarse_rhs.shape[1],), jnp.float32)

    def forward(carry, items):
        lower_block, rhs_block = items
        value = rhs_block - jnp.dot(lower_block, carry, precision=highest)
        return value, value

    _, inner = lax.scan(forward, zero_block, (coarse_lower, coarse_rhs))

    def backward(carry, items):
        upper_block, pivot_block, inner_block = items
        value = jnp.dot(pivot_block, inner_block - jnp.dot(upper_block, carry, precision=highest), precision=highest)
        return value, value

    _, solved = lax.scan(backward, zero_block, (coarse_upper, coarse_pivot, inner), reverse=True)
    return solved


def reference(rhs, fine_blocks, smoother, columns, aggregates, weights, coarse_lower, coarse_upper, coarse_pivot):
    field = jnp.zeros_like(rhs)
    for sweep_index in range(SWEEPS):
        field = sweep_once(fine_blocks, smoother, columns, rhs, field)
    fine_residual = rhs - apply_operator(fine_blocks, field, columns)
    coarse_rhs = jax.ops.segment_sum((weights * fine_residual).reshape(-1), aggregates.reshape(-1), num_segments=NCB * BS).reshape(NCB, BS)
    coarse_solution = coarse_solve(coarse_lower, coarse_upper, coarse_pivot, coarse_rhs)
    field = field + weights * coarse_solution.reshape(-1)[aggregates]
    for sweep_index in range(SWEEPS):
        field = sweep_once(fine_blocks, smoother, columns, rhs, field)
    return field, coarse_solution
```

```python
import functools

import jax
import jax.numpy as jnp
from jax import lax
from jax.experimental import pallas as pl
from jax.experimental.pallas import tpu as pltpu
from jax.sharding import PartitionSpec as P

BS = 128
ROWS = 64
EXT = ROWS + 4
FEXT = ROWS + 8
CHUNK = 8
GROUPS = 32
SMALL = 1024
HALO = 1048

f32 = jnp.float32
highest = lax.Precision.HIGHEST
VMEM = pl.BlockSpec(memory_space=pltpu.VMEM)
SMEM = pl.BlockSpec(memory_space=pltpu.SMEM)
ANY = pl.BlockSpec(memory_space=pl.ANY)
PARAMS = pltpu.CompilerParams(vmem_limit_bytes=48 * 1024 * 1024)


def shape(*dims):
    return jax.ShapeDtypeStruct(dims, f32)


def identity_mask():
    rows = lax.broadcasted_iota(jnp.int32, (BS, BS), 0)
    columns = lax.broadcasted_iota(jnp.int32, (BS, BS), 1)
    return rows == columns


def column_to_row(column, eye):
    return jnp.sum(jnp.where(eye, column, 0.0), axis=0, keepdims=True)


def row_to_column(row, eye):
    return jnp.sum(jnp.where(eye, row, 0.0), axis=1, keepdims=True)


def times_row(matrix, row, eye):
    return column_to_row(jnp.sum(matrix * row, axis=1, keepdims=True), eye)


def product(left, right):
    return jnp.dot(left, right, precision=highest, preferred_element_type=f32)


def prepare_kernel(
    lower, upper, pivot, rhs, weights, aggregates, columns, fine, smoother, lower_hbm, upper_hbm, pivot_hbm,
    maps, inside, to_next, to_previous, line_next, line_previous,
    edge, small, sems,
):
    eye = identity_mask()
    copies = []

    def copy(source, target, index):
        action = pltpu.make_async_copy(source, target, sems.at[index])
        action.start()
        copies.append(action)

    ends = []
    for side, start in ((0, 0), (1, ROWS - 4)):
        action = pltpu.make_async_copy(smoother.at[pl.ds(start, 4)], edge.at[pl.ds(4 * side, 4)], sems.at[side])
        action.start()
        ends.append(action)
    for side, target in ((0, to_previous), (1, to_next)):
        start = side * (ROWS - 2)
        copy(fine.at[pl.ds(start * 3, 6)], target.at[pl.ds(0, 6)], 2 + 2 * side)
        copy(smoother.at[pl.ds(start, 2)], target.at[pl.ds(6, 2)], 3 + 2 * side)
    for side, target in ((0, line_previous), (1, line_next)):
        for at, source in enumerate((lower_hbm, upper_hbm, pivot_hbm)):
            copy(source, target.at[pl.ds(4 * at, 4)], 6 + 3 * side + at)

    forward = [-lower[0]]
    for j in range(1, 4):
        forward.append(-product(lower[j], forward[-1]))
    entering, following = product(pivot[3], forward[3]), -product(pivot[3], upper[3])
    inside[3, 0] = entering
    inside[3, 1] = following
    for j in (2, 1, 0):
        both = product(upper[j], jnp.concatenate([entering, following], axis=1))
        both = product(pivot[j], jnp.concatenate([forward[j] - both[:, :BS], -both[:, BS:]], axis=1))
        entering, following = both[:, :BS], both[:, BS:]
        inside[j, 0] = entering
        inside[j, 1] = following
    odd = lax.axis_index("gy") % 2 == 1
    for at, value in enumerate((forward[3], entering, following)):
        maps[at] = jnp.where(odd, value.T, value)

    for action in ends:
        action.wait()
    lane = lax.broadcasted_iota(jnp.int32, (8, BS), 1)
    for side, target in ((0, to_previous), (1, to_next)):
        start = side * (ROWS - 4)
        for r in range(4):
            small[side, pl.ds(r, 1)] = times_row(edge[4 * side + r], rhs[pl.ds(start + r, 1)], eye)
        small[side, 4:8] = weights[start : start + 4]
        small[side, 8:12] = aggregates[start : start + 4].astype(f32)
        small[side, 12:16] = jnp.zeros((4, BS), f32)
        picked = jnp.zeros((8, BS), jnp.int32)
        for at in range(6):
            picked = jnp.where(lane == at, columns[side * (ROWS - 2) * 3 + at], picked)
        small[side, 16:24] = picked.astype(f32)
    for side, target in ((0, to_previous), (1, to_next)):
        copy(small.at[side], target.at[8, pl.ds(0, 24)], 12 + side)
    for action in copies:
        action.wait()


def load_columns(columns, before_cols, after_cols, j, k, base):
    index = columns[j * 3 + k] - base
    return jnp.clip(index, 0, FEXT - 1)


def presmooth_kernel(
    rhs, weights, aggregates, columns, fine, smoother, before, after,
    shared, first_field, second_field, turned,
    blocks, smooth, halo, residual, halo_columns, sems, chunk_sems, out_sem,
):
    gx = lax.axis_index("gx")
    gy = lax.axis_index("gy")
    eye = identity_mask()
    n_chunks = ROWS // CHUNK
    small = []
    for side, source in ((0, before), (1, after)):
        top = side * (EXT - 2)
        for at, (src, dst) in enumerate((
            (source.at[pl.ds(0, 6)], blocks.at[pl.ds(3 * top, 6)]),
            (source.at[pl.ds(6, 2)], smooth.at[pl.ds(top, 2)]),
            (source.at[8, pl.ds(0, 24)], halo.at[side]),
            (source.at[8, pl.ds(16, 8)], halo_columns.at[side]),
        )):
            action = pltpu.make_async_copy(src, dst, sems.at[side, at])
            action.start()
            small.append(action)

    def smooth_copy(c):
        return pltpu.make_async_copy(
            smoother.at[pl.ds(c * CHUNK, CHUNK)], smooth.at[pl.ds(2 + c * CHUNK, CHUNK)], chunk_sems.at[0, c])

    def block_copy(c):
        return pltpu.make_async_copy(
            fine.at[pl.ds(c * CHUNK * 3, CHUNK * 3)], blocks.at[pl.ds((2 + c * CHUNK) * 3, CHUNK * 3)], chunk_sems.at[1, c])

    for c in range(n_chunks):
        smooth_copy(c).start()
    for c in range(n_chunks):
        block_copy(c).start()
    base = gx * ROWS - 4

    def turn(j):
        smooth[j] = smooth[j].T

    for c in range(n_chunks):
        smooth_copy(c).wait()

        def first_row(r, _):
            n = c * CHUNK + r
            turn(n + 2)
            column = row_to_column(rhs[pl.ds(n, 1)], eye)
            first_field[pl.ds(n + 4, 1)] = jnp.sum(smooth[n + 2] * column, axis=0, keepdims=True)
            return 0

        lax.fori_loop(0, CHUNK, first_row, 0, unroll=4)
    for action in small:
        action.wait()
    for j in (0, 1, EXT - 2, EXT - 1):
        turn(j)
    turned_copy = pltpu.make_async_copy(smooth, turned, out_sem)
    turned_copy.start()
    first_field[0:4] = halo[0, 0:4]
    first_field[FEXT - 4 : FEXT] = halo[1, 0:4]

    def operator_column(field, j, picks):
        total = blocks[3 * j] * field[pl.ds(picks[0], 1)]
        total += blocks[3 * j + 1] * field[pl.ds(picks[1], 1)]
        total += blocks[3 * j + 2] * field[pl.ds(picks[2], 1)]
        return jnp.sum(total, axis=1, keepdims=True)

    def own_picks(n):
        return [jnp.clip(columns[n * 3 + k] - base, 0, FEXT - 1) for k in range(3)]

    def second_row(j, picks):
        column = operator_column(first_field, j, picks)
        change = jnp.sum(smooth[j] * column, axis=0, keepdims=True)
        second_field[pl.ds(j + 2, 1)] = 2.0 * first_field[pl.ds(j + 2, 1)] - change

    second_field[0:2] = jnp.zeros((2, BS), f32)
    second_field[FEXT - 2 : FEXT] = jnp.zeros((2, BS), f32)
    for side in range(2):
        for r in range(2):
            picks = [
                jnp.clip(halo_columns[side, 0, 3 * r + k].astype(jnp.int32) - base, 0, FEXT - 1) for k in range(3)]
            second_row(side * (EXT - 2) + r, picks)
    for c in range(n_chunks):
        block_copy(c).wait()

        def step(r, _):
            n = c * CHUNK + r
            second_row(n + 2, own_picks(n))
            return 0

        lax.fori_loop(0, CHUNK, step, 0, unroll=4)

    def residual_row(n, _):
        column = operator_column(second_field, n + 2, own_picks(n))
        residual[pl.ds(n, 1)] = column_to_row(column, eye)
        return 0

    lax.fori_loop(0, ROWS, residual_row, 0, unroll=4)

    residual[...] = weights[...] * (rhs[...] - residual[...])
    low_block = gy * 4 - 2
    row8 = lax.broadcasted_iota(jnp.int32, (8, BS), 0)
    row128 = lax.broadcasted_iota(jnp.int32, (BS, BS), 0)

    def scatter(n, total):
        index = aggregates[pl.ds(n, 1)]
        block, within = (index >> 7) - low_block, index & 127
        value = jnp.where(row8 == block, residual[pl.ds(n, 1)], 0.0)
        high = value.astype(jnp.bfloat16).astype(f32)
        middle = (value - high).astype(jnp.bfloat16).astype(f32)
        rest = value - high - middle
        parts = jnp.concatenate([high, middle, rest, jnp.zeros_like(rest)], axis=0).astype(jnp.bfloat16)
        hot = jnp.where(row128 == within, 1.0, 0.0).astype(jnp.bfloat16)
        return total + lax.dot_general(parts, hot, (((1,), (1,)), ((), ())), preferred_element_type=f32)

    total = lax.fori_loop(0, ROWS, scatter, jnp.zeros((32, BS), f32), unroll=4)
    shared[0:8] = total[0:8] + total[8:16] + total[16:24]
    shared[8:40] = jnp.zeros((32, BS), f32)
    shared[pl.ds(pl.multiple_of(8 + 8 * gx, 8), 8)] = jnp.concatenate(
        [second_field[4:8], second_field[FEXT - 8 : FEXT - 4]], axis=0)
    turned_copy.wait()


def local_kernel(shared, lower, upper, pivot, previous, following, out):
    eye = identity_mask()
    zero = jnp.zeros((1, BS), f32)

    def row(j):
        return shared[j : j + 1]

    groups = (
        (lambda j: previous[j], lambda j: previous[4 + j], lambda j: previous[8 + j], [zero, zero, row(0), row(1)]),
        (lambda j: lower[j], lambda j: upper[j], lambda j: pivot[j], [row(2), row(3), row(4), row(5)]),
        (lambda j: following[j], lambda j: following[4 + j], lambda j: following[8 + j], [row(6), row(7), zero, zero]),
    )
    inner = [[g[3][0]] for g in groups]
    for j in range(1, 4):
        for g, found in zip(groups, inner):
            found.append(g[3][j] - times_row(g[0](j), found[-1], eye))
    solved = [[None] * 4 for _ in groups]
    for j in (3, 2, 1, 0):
        right = []
        for g, found, x in zip(groups, inner, solved):
            right.append(found[j] if j == 3 else found[j] - times_row(g[1](j), x[j + 1], eye))
        for g, value, x in zip(groups, right, solved):
            x[j] = times_row(g[2](j), value, eye)
    tiles = []
    for found, x in zip(inner, solved):
        tiles += x + [found[3], zero, zero, zero]
    tile = jnp.concatenate(tiles, axis=0)
    for peer in range(GROUPS):
        out[peer] = tile


def correct_kernel(
    parts, shared, first_field, second_field, weights, aggregates, columns, maps, inside, previous, following,
    fine, turned, before, after,
    field_out, coarse_out,
    blocks, smooth, chain, inner_maps, sums, entering, leaving, window, field, next_field, halo, halo_columns,
    sems, chain_sems, chunk_sems,
):
    gx = lax.axis_index("gx")
    gy = lax.axis_index("gy")
    eye = identity_mask()
    n_chunks = ROWS // CHUNK
    step = 8
    chain_copies = {}
    for kind in (0, 1, 2):
        order = range(GROUPS // step) if kind < 2 else reversed(range(GROUPS // step))
        for c in order:
            action = pltpu.make_async_copy(
                maps.at[pl.ds(c * step, step), kind], chain.at[kind, pl.ds(c * step, step)], chain_sems.at[kind, c])
            action.start()
            chain_copies[kind, c] = action
    first = []
    for at, (src, dst) in enumerate((
        (previous.at[pl.ds(12, 4)], inner_maps.at[pl.ds(0, 4)]),
        (inside, inner_maps.at[pl.ds(4, 8)]),
        (following.at[pl.ds(12, 4)], inner_maps.at[pl.ds(12, 4)]),
    )):
        action = pltpu.make_async_copy(src, dst, sems.at[2, at])
        action.start()
        first.append(action)
    halos = []
    for side, source in ((0, before), (1, after)):
        for at, (src, dst) in enumerate((
            (source.at[pl.ds(0, 6)], blocks.at[pl.ds(3 * side * (EXT - 2), 6)]),
            (source.at[8, pl.ds(0, 24)], halo.at[side]),
            (source.at[8, pl.ds(16, 8)], halo_columns.at[side]),
        )):
            action = pltpu.make_async_copy(src, dst, sems.at[side, at])
            action.start()
            halos.append(action)
    whole = pltpu.make_async_copy(turned, smooth, sems.at[2, 3])
    whole.start()

    def block_copy(c):
        return pltpu.make_async_copy(
            fine.at[pl.ds(c * CHUNK * 3, CHUNK * 3)], blocks.at[pl.ds((2 + c * CHUNK) * 3, CHUNK * 3)], chunk_sems.at[c])

    for c in range(n_chunks):
        block_copy(c).start()

    for d in range(GROUPS):
        total = parts[d, 8:16]
        if d + 1 < GROUPS:
            total += parts[d + 1, 0:8]
        if d > 0:
            total += parts[d - 1, 16:24]
        sums[d + 1] = total
    sums[0] = jnp.zeros((8, BS), f32)
    sums[GROUPS + 1] = jnp.zeros((8, BS), f32)

    entering[0:8] = jnp.zeros((8, BS), f32)
    value = jnp.zeros((1, BS), f32)
    heights = []
    for d in range(GROUPS):
        if d % step == 0:
            for kind in (0, 1):
                chain_copies[kind, d // step].wait()
        own, local = sums[d + 1, 4:5], sums[d + 1, 0:1]
        if d % 2 == 0:
            height = jnp.sum(chain[1, d] * value + jnp.where(eye, local, 0.0), axis=1, keepdims=True)
            value = jnp.sum(chain[0, d] * value + jnp.where(eye, own, 0.0), axis=1, keepdims=True)
            entering[d + 1 : d + 2] = column_to_row(value, eye)
        else:
            height = jnp.sum(chain[1, d] * value, axis=0, keepdims=True) + local
            value = jnp.sum(chain[0, d] * value, axis=0, keepdims=True) + own
            entering[d + 1 : d + 2] = value
        heights.append(column_to_row(height, eye) if d % 2 == 0 else height)
    leaving[GROUPS : GROUPS + 8] = jnp.zeros((8, BS), f32)
    value = None
    for d in reversed(range(GROUPS)):
        if d % step == step - 1:
            chain_copies[2, d // step].wait()
        if d == GROUPS - 1:
            value = heights[d]
        elif d % 2 == 0:
            value = jnp.sum(chain[2, d] * value + jnp.where(eye, heights[d], 0.0), axis=1, keepdims=True)
        else:
            value = jnp.sum(chain[2, d] * value, axis=0, keepdims=True) + heights[d]
        leaving[d : d + 1] = column_to_row(value, eye) if d % 2 == 0 else value

    for action in first:
        action.wait()
    for j in range(8):
        offset, block = ((-1, j + 2), (0, j - 2), (1, j - 6))[(j + 2) // 4]
        group = gy + offset
        enter = entering[pl.ds(jnp.maximum(group, 0), 1)]
        leave = leaving[pl.ds(jnp.minimum(group + 1, GROUPS), 1)]
        total = inner_maps[2 * j] * enter + inner_maps[2 * j + 1] * leave
        window[j : j + 1] = column_to_row(jnp.sum(total, axis=1, keepdims=True), eye) + sums[
            group + 1, block : block + 1]
    coarse_out[...] = window[2:6]

    for action in halos:
        action.wait()
    low_block = gy * 4 - 2
    field[4 : ROWS + 4] = second_field[4 : ROWS + 4]
    left = pl.multiple_of(8 + 8 * jnp.maximum(gx - 1, 0), 8)
    right = pl.multiple_of(8 + 8 * jnp.minimum(gx + 1, 3), 8)
    field[0:4] = shared[pl.ds(left, 8)][4:8]
    field[FEXT - 4 : FEXT] = shared[pl.ds(right, 8)][0:4]

    def interpolate(index, weight):
        block, within = (index >> 7) - low_block, index & 127
        total = jnp.zeros(index.shape, f32)
        for j in range(8):
            source = jnp.broadcast_to(window[j : j + 1], index.shape)
            total = jnp.where(block == j, jnp.take_along_axis(source, within, axis=1), total)
        return weight * total

    for at in range(ROWS // 8):
        rows = pl.ds(8 * at, 8)
        field[pl.ds(8 * at + 4, 8)] += interpolate(aggregates[rows], weights[rows])
    for side in range(2):
        index = halo[side, 8:16].astype(jnp.int32)
        value = interpolate(index, jnp.concatenate([halo[side, 4:8], jnp.zeros((4, BS), f32)], axis=0))
        top = side * (FEXT - 4)
        field[top : top + 4] += value[0:4]

    whole.wait()
    base = gx * ROWS - 4

    def swept(source, j, picks):
        total = blocks[3 * j] * source[pl.ds(picks[0], 1)]
        total += blocks[3 * j + 1] * source[pl.ds(picks[1], 1)]
        total += blocks[3 * j + 2] * source[pl.ds(picks[2], 1)]
        column = jnp.sum(total, axis=1, keepdims=True)
        change = jnp.sum(smooth[j] * column, axis=0, keepdims=True)
        return source[pl.ds(j + 2, 1)] + first_field[pl.ds(j + 2, 1)] - change

    def own_picks(n):
        return [jnp.clip(columns[n * 3 + k] - base, 0, FEXT - 1) for k in range(3)]

    next_field[0:2] = jnp.zeros((2, BS), f32)
    next_field[FEXT - 2 : FEXT] = jnp.zeros((2, BS), f32)
    for side in range(2):
        for r in range(2):
            picks = [
                jnp.clip(halo_columns[side, 0, 3 * r + k].astype(jnp.int32) - base, 0, FEXT - 1) for k in range(3)]
            j = side * (EXT - 2) + r
            next_field[pl.ds(j + 2, 1)] = swept(field, j, picks)
    for c in range(n_chunks):
        block_copy(c).wait()

        def third(r, _):
            n = c * CHUNK + r
            next_field[pl.ds(n + 4, 1)] = swept(field, n + 2, own_picks(n))
            return 0

        lax.fori_loop(0, CHUNK, third, 0, unroll=4)

    def fourth(n, _):
        field_out[pl.ds(n, 1)] = swept(next_field, n + 2, own_picks(n))
        return 0

    lax.fori_loop(0, ROWS, fourth, 0, unroll=4)


def per_device(
    rhs, fine_blocks, smoother, columns, aggregates, weights, coarse_lower, coarse_upper, coarse_pivot
):
    rhs, aggregates, weights = rhs[0], aggregates[0], weights[0]
    columns = columns.reshape(ROWS * 3)
    fine = fine_blocks.reshape(ROWS * 3, BS, BS)
    smoother = smoother[0]
    dma = pltpu.SemaphoreType.DMA

    maps, inside, to_next, to_previous, line_next, line_previous = pl.pallas_call(
        prepare_kernel,
        name="prepare",
        out_shape=(
            shape(3, BS, BS), shape(4, 2, BS, BS), shape(9, BS, BS), shape(9, BS, BS),
            shape(12, BS, BS), shape(12, BS, BS),
        ),
        in_specs=[VMEM] * 6 + [SMEM] + [ANY] * 5,
        out_specs=(VMEM, VMEM, ANY, ANY, ANY, ANY),
        scratch_shapes=[pltpu.VMEM((8, BS, BS), f32), pltpu.VMEM((2, 24, BS), f32), dma((16,))],
        compiler_params=PARAMS,
    )(
        coarse_lower, coarse_upper, coarse_pivot, rhs, weights, aggregates, columns, fine, smoother,
        coarse_lower, coarse_upper, coarse_pivot,
    )
    gathered = lax.all_gather(maps, "gy", axis=0)

    up = [(i, i + 1) for i in range(3)]
    down = [(i + 1, i) for i in range(3)]
    before = lax.ppermute(to_next, "gx", up)
    after = lax.ppermute(to_previous, "gx", down)
    line_up = [(i, i + 1) for i in range(GROUPS - 1)]
    line_down = [(i + 1, i) for i in range(GROUPS - 1)]
    inside_flat = inside.reshape(8, BS, BS)
    previous = lax.ppermute(jnp.concatenate([line_next, inside_flat[4:8]], axis=0), "gy", line_up)
    following = lax.ppermute(jnp.concatenate([line_previous, inside_flat[0:4]], axis=0), "gy", line_down)

    shared, first_field, second_field, turned = pl.pallas_call(
        presmooth_kernel,
        name="presmooth",
        out_shape=(shape(40, BS), shape(FEXT, BS), shape(FEXT, BS), shape(EXT, BS, BS)),
        in_specs=[VMEM] * 3 + [SMEM] + [ANY] * 4,
        out_specs=(VMEM, VMEM, VMEM, ANY),
        scratch_shapes=[
            pltpu.VMEM((EXT * 3, BS, BS), f32), pltpu.VMEM((EXT, BS, BS), f32), pltpu.VMEM((2, 24, BS), f32),
            pltpu.VMEM((ROWS, BS), f32), pltpu.SMEM((2, 8, BS), f32),
            dma((2, 4)), dma((2, ROWS // CHUNK)), dma,
        ],
        compiler_params=PARAMS,
    )(rhs, weights, aggregates, columns, fine, smoother, before, after)
    shared = lax.psum(shared, "gx")

    spread = pl.pallas_call(
        local_kernel,
        name="local_solutions",
        out_shape=shape(GROUPS, 24, BS),
        in_specs=[VMEM] * 6,
        out_specs=VMEM,
        compiler_params=PARAMS,
    )(shared, coarse_lower, coarse_upper, coarse_pivot, previous, following)
    parts = lax.all_to_all(spread, "gy", 0, 0)

    field, coarse = pl.pallas_call(
        correct_kernel,
        name="correct",
        out_shape=(shape(ROWS, BS), shape(4, BS)),
        in_specs=[VMEM] * 6 + [SMEM] + [ANY] * 8,
        out_specs=(VMEM, VMEM),
        scratch_shapes=[
            pltpu.VMEM((EXT * 3, BS, BS), f32), pltpu.VMEM((EXT, BS, BS), f32),
            pltpu.VMEM((3, GROUPS, BS, BS), f32), pltpu.VMEM((16, BS, BS), f32),
            pltpu.VMEM((GROUPS + 2, 8, BS), f32), pltpu.VMEM((GROUPS + 8, BS), f32), pltpu.VMEM((GROUPS + 8, BS), f32),
            pltpu.VMEM((8, BS), f32), pltpu.VMEM((FEXT, BS), f32), pltpu.VMEM((FEXT, BS), f32),
            pltpu.VMEM((2, 24, BS), f32), pltpu.SMEM((2, 8, BS), f32),
            dma((3, 4)), dma((3, 4)), dma((ROWS // CHUNK,)),
        ],
        compiler_params=PARAMS,
    )(
        parts, shared, first_field, second_field, weights, aggregates, columns, gathered, inside_flat,
        previous, following, fine, turned, before, after,
    )
    return (field[None], coarse)


def solution(mesh):
    return jax.shard_map(
        per_device,
        mesh=mesh,
        in_specs=(
            P("gy", "gx", None),
            P("gy", "gx", None, None, None),
            P("gy", "gx", None, None),
            P("gy", "gx", None),
            P("gy", "gx", None),
            P("gy", "gx", None),
            P("gy", None, None),
            P("gy", None, None),
            P("gy", None, None),
        ),
        out_specs=(P("gy", "gx", None), P("gy", None)),
        check_vma=False,
    )
```

```python
import jax
import jax.numpy as jnp
from jax import lax
from jax.experimental import pallas as pl
from jax.experimental.pallas import tpu as pltpu
from jax.sharding import PartitionSpec as P

BS = 128
ROWS = 64
FEXT = ROWS + 8
CHUNK = 8
LOWER, UPPER, PIVOT, INSIDE = 0, 4, 8, 12
GROUPS = 32
f32 = jnp.float32
VMEM = pl.BlockSpec(memory_space=pltpu.VMEM)
SMEM = pl.BlockSpec(memory_space=pltpu.SMEM)
HBM = pl.BlockSpec(memory_space=pltpu.HBM)


def grant(mib):
    return pltpu.CompilerParams(vmem_limit_bytes=mib * 1024 * 1024)


def shape(*dims):
    return jax.ShapeDtypeStruct(dims, f32)


def identity_mask():
    rows = lax.broadcasted_iota(jnp.int32, (BS, BS), 0)
    columns = lax.broadcasted_iota(jnp.int32, (BS, BS), 1)
    return rows == columns


def column_to_row(column, eye):
    return jnp.sum(jnp.where(eye, column, 0.0), axis=0, keepdims=True)


def times_row(matrix, row, eye):
    return column_to_row(jnp.sum(matrix * row, axis=1, keepdims=True), eye)


def halves(value):
    high = value.astype(jnp.bfloat16)
    return high, (value - high.astype(f32)).astype(jnp.bfloat16)


def product(left, right):
    left_high, left_low = halves(left)
    right_high, right_low = halves(right)
    return jnp.dot(
        jnp.concatenate([left_high, left_high, left_low], axis=1),
        jnp.concatenate([right_high, right_low, right_high], axis=0),
        preferred_element_type=f32,
    )


def maps_kernel(lower, upper, pivot, maps_out, mine_out, maps, mine, sems, out_sems):
    coarse = [
        pltpu.make_async_copy(source, mine.at[pl.ds(4 * at, 4)], sems.at[at])
        for at, source in enumerate((lower, upper, pivot))
    ]
    for action in coarse:
        action.start()
    coarse[0].wait()
    forward = [-mine[LOWER]]
    for j in range(1, 4):
        forward.append(-product(mine[LOWER + j], forward[-1]))
    for action in coarse[1:]:
        action.wait()
    both = product(mine[PIVOT + 3], jnp.concatenate([forward[3], -mine[UPPER + 3]], axis=1))
    for j in (3, 2, 1, 0):
        if j < 3:
            both = product(mine[UPPER + j], both)
            both = product(mine[PIVOT + j], jnp.concatenate([forward[j] - both[:, :BS], -both[:, BS:]], axis=1))
        mine[INSIDE + 2 * j] = both[:, :BS]
        mine[INSIDE + 2 * j + 1] = both[:, BS:]
    odd = lax.axis_index("gy") % 2 == 1
    for at, value in enumerate((forward[3], both[:, :BS], both[:, BS:])):
        maps[at] = jnp.where(odd, value.T, value)
    sent = [
        pltpu.make_async_copy(maps, maps_out, out_sems.at[0]),
        pltpu.make_async_copy(mine, mine_out, out_sems.at[1]),
    ]
    for action in sent:
        action.start()
    for action in sent:
        action.wait()


def pack_kernel(
    rhs, weights, aggregates, columns, fine, smoother,
    to_previous, to_next,
    packed, edge, ends, indices, sems, out_sems,
):
    eye = identity_mask()

    def start(source, target, *at):
        action = pltpu.make_async_copy(source, target, sems.at[at])
        action.start()
        return action

    near, far = [], []
    for side in range(2):
        top = side * (ROWS - 8)
        near.append(start(smoother.at[pl.ds(side * (ROWS - 4), 4)], edge.at[side], side, 0))
        near.append(start(rhs.at[pl.ds(top, 8)], ends.at[side, 0], side, 1))
        near.append(start(weights.at[pl.ds(top, 8)], ends.at[side, 1], side, 2))
        near.append(start(aggregates.at[pl.ds(top, 8)], indices.at[side], side, 3))
    for side in range(2):
        far.append(start(fine.at[pl.ds(side * (ROWS - 2) * 3, 6)], packed.at[side, pl.ds(0, 6)], side, 4))
    for action in near:
        action.wait()
    lane = lax.broadcasted_iota(jnp.int32, (8, BS), 1)
    for side in range(2):
        top = 4 * side
        packed[side, 6] = edge[side, 2 * side].T
        packed[side, 7] = edge[side, 2 * side + 1].T
        for r in range(4):
            packed[side, 8, r : r + 1] = times_row(edge[side, r], ends[side, 0, top + r : top + r + 1], eye)
        packed[side, 8, 4:8] = ends[side, 1, top : top + 4]
        packed[side, 8, 8:12] = indices[side, top : top + 4].astype(f32)
        packed[side, 8, 12:16] = jnp.zeros((4, BS), f32)
        picked = jnp.zeros((8, BS), jnp.int32)
        for r in range(2):
            for k in range(3):
                picked = jnp.where(lane == 3 * r + k, columns[k, 0, side * (ROWS - 2) + r], picked)
        packed[side, 8, 16:24] = picked.astype(f32)
        packed[side, 8, 24:BS] = jnp.zeros((BS - 24, BS), f32)
    for action in far:
        action.wait()
    sent = [
        pltpu.make_async_copy(packed.at[side], target, out_sems.at[side])
        for side, target in enumerate((to_previous, to_next))
    ]
    for action in sent:
        action.start()
    for action in sent:
        action.wait()


def first_kernel(rhs, smoother, turned, first, smooth, rhs_rows, sems, rhs_sem):
    eye = identity_mask()
    n_chunks = ROWS // CHUNK

    def smooth_copy(c):
        rows = pl.ds(c * CHUNK, CHUNK)
        return pltpu.make_async_copy(smoother.at[rows], smooth.at[rows], sems.at[c])

    small = pltpu.make_async_copy(rhs, rhs_rows, rhs_sem)
    small.start()
    for c in range(n_chunks):
        smooth_copy(c).start()
    small.wait()
    for c in range(n_chunks):
        smooth_copy(c).wait()

        def row(r, _):
            n = c * CHUNK + r
            block = smooth[n]
            column = jnp.sum(block * rhs_rows[pl.ds(n, 1)], axis=1, keepdims=True)
            first[pl.ds(n, 1)] = column_to_row(column, eye)
            turned[n] = block.T
            return 0

        lax.fori_loop(0, CHUNK, row, 0, unroll=8)


def change_row(blocks, at, turned_block, source, picks):
    total = blocks[at] * source[pl.ds(picks[0], 1)]
    total += blocks[at + 1] * source[pl.ds(picks[1], 1)]
    total += blocks[at + 2] * source[pl.ds(picks[2], 1)]
    column = jnp.sum(total, axis=1, keepdims=True)
    if turned_block is None:
        return column
    return jnp.sum(turned_block * column, axis=0, keepdims=True)


def picks_of(columns, n, base):
    return [jnp.clip(columns[k, 0, n] - base, 0, FEXT - 1) for k in range(3)]


def halo_picks(halo_columns, side, r, base):
    return [
        jnp.clip(halo_columns[side, 0, 3 * r + k].astype(jnp.int32) - base, 0, FEXT - 1) for k in range(3)]


def presmooth_kernel(
    rhs, weights, aggregates, columns, fine, turned, first, before, after,
    shared, first_field, second_own,
    blocks, second_field, residual, rows, indices, halo_columns, sems, block_sems,
):
    gx = lax.axis_index("gx")
    gy = lax.axis_index("gy")
    eye = identity_mask()
    copies = [
        pltpu.make_async_copy(before.at[8, pl.ds(16, 8)], halo_columns.at[0], sems.at[0]),
        pltpu.make_async_copy(after.at[8, pl.ds(16, 8)], halo_columns.at[1], sems.at[1]),
        pltpu.make_async_copy(rhs, rows.at[0], sems.at[2]),
        pltpu.make_async_copy(weights, rows.at[1], sems.at[3]),
        pltpu.make_async_copy(aggregates, indices, sems.at[4]),
    ]
    n_chunks = ROWS // CHUNK

    def block_copy(c):
        part = pl.ds(c * CHUNK * 3, CHUNK * 3)
        return pltpu.make_async_copy(fine.at[part], blocks.at[part], block_sems.at[c])

    for c in range(n_chunks):
        block_copy(c).start()
    for action in copies:
        action.start()
    base = gx * ROWS - 4
    first_field[4 : ROWS + 4] = first[...]
    first_field[0:4] = before[8, 0:4]
    first_field[FEXT - 4 : FEXT] = after[8, 0:4]
    second_field[0:2] = jnp.zeros((2, BS), f32)
    second_field[FEXT - 2 : FEXT] = jnp.zeros((2, BS), f32)

    def second_row(n, _):
        change = change_row(blocks, 3 * n, turned[n], first_field, picks_of(columns, n, base))
        second_field[pl.ds(n + 4, 1)] = 2.0 * first_field[pl.ds(n + 4, 1)] - change
        return 0

    for c in range(n_chunks):
        block_copy(c).wait()
        lax.fori_loop(c * CHUNK, c * CHUNK + CHUNK, second_row, 0, unroll=8)
    copies[0].wait()
    copies[1].wait()
    for side, source in ((0, before), (1, after)):
        for r in range(2):
            at = side * (ROWS + 2) + 2 + r
            change = change_row(
                source, 3 * r, source[6 + r], first_field, halo_picks(halo_columns, side, r, base))
            second_field[at : at + 1] = 2.0 * first_field[at : at + 1] - change
    second_own[...] = second_field[4 : ROWS + 4]

    def residual_row(n, _):
        column = change_row(blocks, 3 * n, None, second_field, picks_of(columns, n, base))
        residual[pl.ds(n, 1)] = column_to_row(column, eye)
        return 0

    lax.fori_loop(0, ROWS, residual_row, 0, unroll=8)
    for action in copies[2:]:
        action.wait()
    residual[...] = rows[1] * (rows[0] - residual[...])
    low_block = gy * 4 - 2
    row8 = lax.broadcasted_iota(jnp.int32, (8, BS), 0)
    row128 = lax.broadcasted_iota(jnp.int32, (BS, BS), 0)

    def scatter(n, total):
        index = indices[pl.ds(n, 1)]
        block, within = (index >> 7) - low_block, index & 127
        value = jnp.where(row8 == block, residual[pl.ds(n, 1)], 0.0)
        high = value.astype(jnp.bfloat16).astype(f32)
        parts = jnp.concatenate([high, value - high], axis=0).astype(jnp.bfloat16)
        hot = jnp.where(row128 == within, 1.0, 0.0).astype(jnp.bfloat16)
        return total + lax.dot_general(parts, hot, (((1,), (1,)), ((), ())), preferred_element_type=f32)

    total = lax.fori_loop(0, ROWS, scatter, jnp.zeros((16, BS), f32), unroll=8)
    shared[0:8] = total[0:8] + total[8:16]
    shared[8:40] = jnp.zeros((32, BS), f32)
    shared[pl.ds(pl.multiple_of(8 + 8 * gx, 8), 8)] = jnp.concatenate(
        [second_field[4:8], second_field[FEXT - 8 : FEXT - 4]], axis=0)


def local_kernel(shared, mine, previous, following, out):
    eye = identity_mask()
    zero = jnp.zeros((1, BS), f32)
    own = [shared[j : j + 1] for j in range(8)]
    groups = (
        (previous, [zero, zero, own[0], own[1]]),
        (mine, own[2:6]),
        (following, [own[6], own[7], zero, zero]),
    )
    inner = [[right[0]] for _, right in groups]
    for j in range(1, 4):
        for (source, right), found in zip(groups, inner):
            found.append(right[j] - times_row(source[LOWER + j], found[-1], eye))
    solved = [[None] * 4 for _ in groups]
    for j in (3, 2, 1, 0):
        held = []
        for (source, _), found, x in zip(groups, inner, solved):
            held.append(found[j] if j == 3 else found[j] - times_row(source[UPPER + j], x[j + 1], eye))
        for (source, _), value, x in zip(groups, held, solved):
            x[j] = times_row(source[PIVOT + j], value, eye)
    tiles = []
    for found, x in zip(inner, solved):
        tiles += x + [found[3], zero, zero, zero]
    tile = jnp.concatenate(tiles, axis=0)
    for peer in range(GROUPS):
        out[peer] = tile


def correct_kernel(
    parts_hbm, shared, first_field, second_own, weights, aggregates, columns, maps, mine, previous, following,
    fine, turned_hbm, before_hbm, after_hbm,
    field_out, coarse_out,
    parts, chain, inside, blocks, turned, halo, sums, entering, leaving, window, field, next_field, halo_columns,
    weight_rows, indices, sems, chain_sems, block_sems,
):
    gx = lax.axis_index("gx")
    gy = lax.axis_index("gy")
    eye = identity_mask()
    step = 8
    chain_copies = {}
    arrived = pltpu.make_async_copy(parts_hbm, parts, sems.at[4])
    arrived.start()
    for kind in (0, 1, 2):
        order = range(GROUPS // step) if kind < 2 else reversed(range(GROUPS // step))
        for c in order:
            action = pltpu.make_async_copy(
                maps.at[pl.ds(c * step, step), kind], chain.at[kind, pl.ds(c * step, step)], chain_sems.at[kind, c])
            action.start()
            chain_copies[kind, c] = action
    copies = [
        pltpu.make_async_copy(previous.at[pl.ds(INSIDE + 4, 4)], inside.at[pl.ds(0, 4)], sems.at[5]),
        pltpu.make_async_copy(mine.at[pl.ds(INSIDE, 8)], inside.at[pl.ds(4, 8)], sems.at[6]),
        pltpu.make_async_copy(following.at[pl.ds(INSIDE, 4)], inside.at[pl.ds(12, 4)], sems.at[7]),
        pltpu.make_async_copy(before_hbm.at[8, pl.ds(16, 8)], halo_columns.at[0], sems.at[0]),
        pltpu.make_async_copy(after_hbm.at[8, pl.ds(16, 8)], halo_columns.at[1], sems.at[1]),
        pltpu.make_async_copy(weights, weight_rows, sems.at[2]),
        pltpu.make_async_copy(aggregates, indices, sems.at[3]),
        pltpu.make_async_copy(before_hbm, halo.at[0], sems.at[8]),
        pltpu.make_async_copy(after_hbm, halo.at[1], sems.at[9]),
    ]
    for action in copies:
        action.start()
    whole = [pltpu.make_async_copy(turned_hbm, turned, sems.at[10])]
    for c in range(4):
        rows = pl.ds(c * (ROWS * 3 // 4), ROWS * 3 // 4)
        whole.append(pltpu.make_async_copy(fine.at[rows], blocks.at[rows], block_sems.at[c]))
    for action in whole:
        action.start()
    before, after = halo.at[0], halo.at[1]
    arrived.wait()

    for d in range(GROUPS):
        total = parts[d, 8:16]
        if d + 1 < GROUPS:
            total += parts[d + 1, 0:8]
        if d > 0:
            total += parts[d - 1, 16:24]
        sums[d + 1] = total
    sums[0] = jnp.zeros((8, BS), f32)
    sums[GROUPS + 1] = jnp.zeros((8, BS), f32)

    entering[0:8] = jnp.zeros((8, BS), f32)
    value = jnp.zeros((1, BS), f32)
    heights = []
    for d in range(GROUPS):
        if d % step == 0:
            for kind in (0, 1):
                chain_copies[kind, d // step].wait()
        own, local = sums[d + 1, 4:5], sums[d + 1, 0:1]
        if d % 2 == 0:
            height = jnp.sum(chain[1, d] * value + jnp.where(eye, local, 0.0), axis=1, keepdims=True)
            value = jnp.sum(chain[0, d] * value + jnp.where(eye, own, 0.0), axis=1, keepdims=True)
            entering[d + 1 : d + 2] = column_to_row(value, eye)
        else:
            height = jnp.sum(chain[1, d] * value, axis=0, keepdims=True) + local
            value = jnp.sum(chain[0, d] * value, axis=0, keepdims=True) + own
            entering[d + 1 : d + 2] = value
        heights.append(column_to_row(height, eye) if d % 2 == 0 else height)
    leaving[GROUPS : GROUPS + 8] = jnp.zeros((8, BS), f32)
    value = None
    for d in reversed(range(GROUPS)):
        if d % step == step - 1:
            chain_copies[2, d // step].wait()
        if d == GROUPS - 1:
            value = heights[d]
        elif d % 2 == 0:
            value = jnp.sum(chain[2, d] * value + jnp.where(eye, heights[d], 0.0), axis=1, keepdims=True)
        else:
            value = jnp.sum(chain[2, d] * value, axis=0, keepdims=True) + heights[d]
        leaving[d : d + 1] = column_to_row(value, eye) if d % 2 == 0 else value

    for action in copies[:3]:
        action.wait()
    for j in range(8):
        offset, block = ((-1, j + 2), (0, j - 2), (1, j - 6))[(j + 2) // 4]
        group = gy + offset
        enter = entering[pl.ds(jnp.maximum(group, 0), 1)]
        leave = leaving[pl.ds(jnp.minimum(group + 1, GROUPS), 1)]
        total = inside[2 * j] * enter + inside[2 * j + 1] * leave
        window[j : j + 1] = column_to_row(jnp.sum(total, axis=1, keepdims=True), eye) + sums[
            group + 1, block : block + 1]
    coarse_out[...] = window[2:6]

    for action in copies[3:]:
        action.wait()
    low_block = gy * 4 - 2
    field[4 : ROWS + 4] = second_own[...]
    left = pl.multiple_of(8 + 8 * jnp.maximum(gx - 1, 0), 8)
    right = pl.multiple_of(8 + 8 * jnp.minimum(gx + 1, 3), 8)
    field[0:4] = shared[pl.ds(left, 8)][4:8]
    field[FEXT - 4 : FEXT] = shared[pl.ds(right, 8)][0:4]

    def interpolate(index, weight):
        block, within = (index >> 7) - low_block, index & 127
        total = jnp.zeros(index.shape, f32)
        for j in range(8):
            source = jnp.broadcast_to(window[j : j + 1], index.shape)
            total = jnp.where(block == j, jnp.take_along_axis(source, within, axis=1), total)
        return weight * total

    for at in range(ROWS // 8):
        rows = pl.ds(8 * at, 8)
        field[pl.ds(8 * at + 4, 8)] += interpolate(indices[rows], weight_rows[rows])
    for top, source in ((0, before), (FEXT - 4, after)):
        index = source[8, 8:16].astype(jnp.int32)
        weight = jnp.concatenate([source[8, 4:8], jnp.zeros((4, BS), f32)], axis=0)
        field[top : top + 4] += interpolate(index, weight)[0:4]

    base = gx * ROWS - 4
    next_field[0:2] = jnp.zeros((2, BS), f32)
    next_field[FEXT - 2 : FEXT] = jnp.zeros((2, BS), f32)
    for action in whole:
        action.wait()

    def third(n, _):
        change = change_row(blocks, 3 * n, turned[n], field, picks_of(columns, n, base))
        rows = pl.ds(n + 4, 1)
        next_field[rows] = field[rows] + first_field[rows] - change
        return 0

    lax.fori_loop(0, ROWS, third, 0, unroll=8)
    for side, source in ((0, before), (1, after)):
        for r in range(2):
            at = side * (ROWS + 2) + 2 + r
            change = change_row(source, 3 * r, source[6 + r], field, halo_picks(halo_columns, side, r, base))
            next_field[at : at + 1] = field[at : at + 1] + first_field[at : at + 1] - change

    def fourth(n, _):
        change = change_row(blocks, 3 * n, turned[n], next_field, picks_of(columns, n, base))
        rows = pl.ds(n + 4, 1)
        field_out[pl.ds(n, 1)] = next_field[rows] + first_field[rows] - change
        return 0

    lax.fori_loop(0, ROWS, fourth, 0, unroll=8)


def per_device(
    rhs, fine_blocks, smoother, columns, aggregates, weights, coarse_lower, coarse_upper, coarse_pivot
):
    rhs, aggregates, weights, columns, smoother = rhs[0], aggregates[0], weights[0], columns.transpose(2, 0, 1), smoother[0]
    fine = fine_blocks.reshape(ROWS * 3, BS, BS)
    dma = pltpu.SemaphoreType.DMA

    maps, mine = pl.pallas_call(
        maps_kernel,
        name="maps",
        out_shape=(shape(3, BS, BS), shape(20, BS, BS)),
        in_specs=[HBM] * 3,
        out_specs=(HBM, HBM),
        scratch_shapes=[pltpu.VMEM((3, BS, BS), f32), pltpu.VMEM((20, BS, BS), f32), dma((3,)), dma((2,))],
        compiler_params=grant(58),
    )(coarse_lower, coarse_upper, coarse_pivot)
    gathered = lax.all_gather(maps, "gy", axis=0)

    to_previous, to_next = pl.pallas_call(
        pack_kernel,
        name="pack",
        out_shape=(shape(9, BS, BS), shape(9, BS, BS)),
        in_specs=[HBM] * 3 + [SMEM] + [HBM] * 2,
        out_specs=(HBM, HBM),
        scratch_shapes=[
            pltpu.VMEM((2, 9, BS, BS), f32), pltpu.VMEM((2, 4, BS, BS), f32), pltpu.VMEM((2, 2, 8, BS), f32),
            pltpu.VMEM((2, 8, BS), jnp.int32), dma((2, 5)), dma((2,)),
        ],
        compiler_params=grant(58),
    )(rhs, weights, aggregates, columns, fine, smoother)
    before = lax.ppermute(to_next, "gx", [(i, i + 1) for i in range(3)])
    after = lax.ppermute(to_previous, "gx", [(i + 1, i) for i in range(3)])

    turned, first = pl.pallas_call(
        first_kernel,
        name="first",
        out_shape=(shape(ROWS, BS, BS), shape(ROWS, BS)),
        in_specs=[HBM] * 2,
        out_specs=(VMEM, VMEM),
        scratch_shapes=[pltpu.VMEM((ROWS, BS, BS), f32), pltpu.VMEM((ROWS, BS), f32), dma((ROWS // CHUNK,)), dma],
        compiler_params=grant(56),
    )(rhs, smoother)

    shared, first_field, second_own = pl.pallas_call(
        presmooth_kernel,
        name="presmooth",
        out_shape=(shape(40, BS), shape(FEXT, BS), shape(ROWS, BS)),
        in_specs=[HBM] * 3 + [SMEM] + [HBM] + [VMEM] * 4,
        out_specs=(VMEM, VMEM, VMEM),
        scratch_shapes=[
            pltpu.VMEM((ROWS * 3, BS, BS), f32), pltpu.VMEM((FEXT, BS), f32), pltpu.VMEM((ROWS, BS), f32),
            pltpu.VMEM((2, ROWS, BS), f32), pltpu.VMEM((ROWS, BS), jnp.int32), pltpu.SMEM((2, 8, BS), f32),
            dma((5,)), dma((ROWS // CHUNK,)),
        ],
        compiler_params=grant(52),
    )(rhs, weights, aggregates, columns, fine, turned, first, before, after)
    previous = lax.ppermute(mine, "gy", [(i, i + 1) for i in range(GROUPS - 1)])
    following = lax.ppermute(mine, "gy", [(i + 1, i) for i in range(GROUPS - 1)])
    for bit in (1, 2):
        shared = shared + lax.ppermute(shared, "gx", [(i, i ^ bit) for i in range(4)])

    spread = pl.pallas_call(
        local_kernel,
        name="local_solutions",
        out_shape=shape(GROUPS, 24, BS),
        in_specs=[VMEM] * 4,
        out_specs=VMEM,
        compiler_params=grant(40),
    )(shared, mine, previous, following)
    parts = lax.all_to_all(spread, "gy", 0, 0)

    field, coarse = pl.pallas_call(
        correct_kernel,
        name="correct",
        out_shape=(shape(ROWS, BS), shape(4, BS)),
        in_specs=[HBM] + [VMEM] * 3 + [HBM] * 2 + [SMEM] + [HBM] * 8,
        out_specs=(VMEM, VMEM),
        scratch_shapes=[
            pltpu.VMEM((GROUPS, 24, BS), f32), pltpu.VMEM((3, GROUPS, BS, BS), f32), pltpu.VMEM((16, BS, BS), f32),
            pltpu.VMEM((ROWS * 3, BS, BS), f32), pltpu.VMEM((ROWS, BS, BS), f32), pltpu.VMEM((2, 9, BS, BS), f32),
            pltpu.VMEM((GROUPS + 2, 8, BS), f32),
            pltpu.VMEM((GROUPS + 8, BS), f32), pltpu.VMEM((GROUPS + 8, BS), f32), pltpu.VMEM((8, BS), f32),
            pltpu.VMEM((FEXT, BS), f32), pltpu.VMEM((FEXT, BS), f32), pltpu.SMEM((2, 8, BS), f32),
            pltpu.VMEM((ROWS, BS), f32), pltpu.VMEM((ROWS, BS), jnp.int32), dma((11,)), dma((3, 4)), dma((4,)),
        ],
        compiler_params=grant(58),
    )(
        parts, shared, first_field, second_own, weights, aggregates, columns, gathered, mine, previous, following,
        fine, turned, before, after,
    )
    return (field[None], coarse)


def solution(mesh):
    return jax.shard_map(
        per_device,
        mesh=mesh,
        in_specs=(
            P("gy", "gx", None),
            P("gy", "gx", None, None, None),
            P("gy", "gx", None, None),
            P("gy", "gx", None),
            P("gy", "gx", None),
            P("gy", "gx", None),
            P("gy", None, None),
            P("gy", None, None),
            P("gy", None, None),
        ),
        out_specs=(P("gy", "gx", None), P("gy", None)),
        check_vma=False,
    )
```

```python
import jax
import jax.numpy as jnp
from jax import lax
from jax.experimental import pallas as pl
from jax.experimental.pallas import tpu as pltpu
from jax.sharding import PartitionSpec as P

BS = 128
ROWS = 64
FEXT = ROWS + 8
CHUNK = 8
LOWER, UPPER, PIVOT, INSIDE = 0, 4, 8, 12
GROUPS = 32
TURNED, SMALL, HALO = 768, 1024, 1048
f32 = jnp.float32
VMEM = pl.BlockSpec(memory_space=pltpu.VMEM)
SMEM = pl.BlockSpec(memory_space=pltpu.SMEM)
HBM = pl.BlockSpec(memory_space=pltpu.HBM)


def grant(mib):
    return pltpu.CompilerParams(vmem_limit_bytes=mib * 1024 * 1024)


def shape(*dims):
    return jax.ShapeDtypeStruct(dims, f32)


def identity_mask():
    rows = lax.broadcasted_iota(jnp.int32, (BS, BS), 0)
    columns = lax.broadcasted_iota(jnp.int32, (BS, BS), 1)
    return rows == columns


def column_to_row(column, eye):
    return jnp.sum(jnp.where(eye, column, 0.0), axis=0, keepdims=True)


def times_row(matrix, row, eye):
    return column_to_row(jnp.sum(matrix * row, axis=1, keepdims=True), eye)


def halves(value):
    high = value.astype(jnp.bfloat16)
    return high, (value - high.astype(f32)).astype(jnp.bfloat16)


def product(left, right):
    left_high, left_low = halves(left)
    right_high, right_low = halves(right)
    return jnp.dot(
        jnp.concatenate([left_high, left_high, left_low], axis=1),
        jnp.concatenate([right_high, right_low, right_high], axis=0),
        preferred_element_type=f32,
    )


def maps_kernel(lower, upper, pivot, maps_out, mine_out, maps, mine, sems, out_sems):
    coarse = [
        pltpu.make_async_copy(source, mine.at[pl.ds(4 * at, 4)], sems.at[at])
        for at, source in enumerate((lower, upper, pivot))
    ]
    for action in coarse:
        action.start()
    coarse[0].wait()
    forward = [-mine[LOWER]]
    for j in range(1, 4):
        forward.append(-product(mine[LOWER + j], forward[-1]))
    for action in coarse[1:]:
        action.wait()
    both = product(mine[PIVOT + 3], jnp.concatenate([forward[3], -mine[UPPER + 3]], axis=1))
    for j in (3, 2, 1, 0):
        if j < 3:
            both = product(mine[UPPER + j], both)
            both = product(mine[PIVOT + j], jnp.concatenate([forward[j] - both[:, :BS], -both[:, BS:]], axis=1))
        mine[INSIDE + 2 * j] = both[:, :BS]
        mine[INSIDE + 2 * j + 1] = both[:, BS:]
    odd = lax.axis_index("gy") % 2 == 1
    for at, value in enumerate((forward[3], both[:, :BS], both[:, BS:])):
        maps[at] = jnp.where(odd, value.T, value)
    sent = [
        pltpu.make_async_copy(maps, maps_out, out_sems.at[0]),
        pltpu.make_async_copy(mine, mine_out, out_sems.at[1]),
    ]
    for action in sent:
        action.start()
    for action in sent:
        action.wait()


def pack_kernel(
    rhs, weights, aggregates, columns, fine, smoother, mine,
    to_previous, to_next, mine_out,
    packed, edge, ends, indices, sems, out_sems,
):
    eye = identity_mask()

    def start(source, target, *at):
        action = pltpu.make_async_copy(source, target, sems.at[at])
        action.start()
        return action

    near, far = [], []
    for side in range(2):
        top = side * (ROWS - 8)
        near.append(start(smoother.at[pl.ds(side * (ROWS - 4), 4)], edge.at[side], side, 0))
        near.append(start(rhs.at[pl.ds(top, 8)], ends.at[side, 0], side, 1))
        near.append(start(weights.at[pl.ds(top, 8)], ends.at[side, 1], side, 2))
        near.append(start(aggregates.at[pl.ds(top, 8)], indices.at[side], side, 3))
    for side in range(2):
        far.append(start(fine.at[pl.ds(side * (ROWS - 2) * 3 * BS, TURNED)], packed.at[side, pl.ds(0, TURNED)], side, 4))
    for action in near:
        action.wait()
    lane = lax.broadcasted_iota(jnp.int32, (8, BS), 1)
    for side in range(2):
        top = 4 * side
        packed[side, TURNED : TURNED + BS] = edge[side, 2 * side].T
        packed[side, TURNED + BS : SMALL] = edge[side, 2 * side + 1].T
        for r in range(4):
            packed[side, SMALL + r : SMALL + r + 1] = times_row(
                edge[side, r], ends[side, 0, top + r : top + r + 1], eye)
        packed[side, SMALL + 4 : SMALL + 8] = ends[side, 1, top : top + 4]
        packed[side, SMALL + 8 : SMALL + 12] = indices[side, top : top + 4].astype(f32)
        packed[side, SMALL + 12 : SMALL + 16] = jnp.zeros((4, BS), f32)
        picked = jnp.zeros((8, BS), jnp.int32)
        for r in range(2):
            for k in range(3):
                picked = jnp.where(lane == 3 * r + k, columns[k, 0, side * (ROWS - 2) + r], picked)
        packed[side, SMALL + 16 : HALO] = picked.astype(f32)
    for action in far:
        action.wait()
    sent = [
        pltpu.make_async_copy(packed.at[side], target, out_sems.at[side])
        for side, target in enumerate((to_previous, to_next))
    ]
    for action in sent:
        action.start()
    for action in sent:
        action.wait()


def change_row(blocks, turned_block, source, picks):
    total = blocks[0] * source[pl.ds(picks[0], 1)]
    total += blocks[1] * source[pl.ds(picks[1], 1)]
    total += blocks[2] * source[pl.ds(picks[2], 1)]
    column = jnp.sum(total, axis=1, keepdims=True)
    if turned_block is None:
        return column
    return jnp.sum(turned_block * column, axis=0, keepdims=True)


def own_blocks(blocks, n):
    return [blocks[3 * n + k] for k in range(3)]


def halo_change(halo, r, source, picks):
    blocks = [halo[(3 * r + k) * BS : (3 * r + k + 1) * BS] for k in range(3)]
    return change_row(blocks, halo[TURNED + r * BS : TURNED + (r + 1) * BS], source, picks)


def picks_of(columns, n, base):
    return [jnp.clip(columns[k, 0, n] - base, 0, FEXT - 1) for k in range(3)]


def halo_picks(halo_columns, side, r, base):
    return [
        jnp.clip(halo_columns[side, 0, 3 * r + k].astype(jnp.int32) - base, 0, FEXT - 1) for k in range(3)]


def scattered(total, value, index, low_block):
    row8 = lax.broadcasted_iota(jnp.int32, (8, BS), 0)
    row128 = lax.broadcasted_iota(jnp.int32, (BS, BS), 0)
    block, within = (index >> 7) - low_block, index & 127
    value = jnp.where(row8 == block, value, 0.0)
    high = value.astype(jnp.bfloat16).astype(f32)
    parts = jnp.concatenate([high, value - high], axis=0).astype(jnp.bfloat16)
    hot = jnp.where(row128 == within, 1.0, 0.0).astype(jnp.bfloat16)
    return total + lax.dot_general(parts, hot, (((1,), (1,)), ((), ())), preferred_element_type=f32)


def interior_kernel(
    rhs, weights, aggregates, columns, fine, smoother, packed,
    turned_out, first_out, second_out, total_out,
    blocks, smooth, turned, first, second, residual, rows, indices, sems, small_sems, out_sems,
):
    gx = lax.axis_index("gx")
    low_block = lax.axis_index("gy") * 4 - 2
    eye = identity_mask()
    n_chunks = ROWS // CHUNK
    small = [
        pltpu.make_async_copy(rhs, rows.at[0], small_sems.at[0]),
        pltpu.make_async_copy(weights, rows.at[1], small_sems.at[1]),
        pltpu.make_async_copy(aggregates, indices, small_sems.at[2]),
    ]
    for action in small:
        action.start()

    def fetch(c):
        part = pl.ds(c * CHUNK, CHUNK)
        return pltpu.make_async_copy(smoother.at[part], smooth.at[part], sems.at[0, c])

    def block_copy(c):
        part = pl.ds(c * CHUNK * 3, CHUNK * 3)
        return pltpu.make_async_copy(fine.at[part], blocks.at[part], sems.at[1, c])

    def store(c):
        part = pl.ds(c * CHUNK, CHUNK)
        return pltpu.make_async_copy(turned.at[part], turned_out.at[part], out_sems.at[c])

    for c in range(n_chunks):
        fetch(c).start()
    for c in range(n_chunks):
        block_copy(c).start()
    for action in small:
        action.wait()

    def first_row(n, _):
        block = smooth[n]
        column = jnp.sum(block * rows[0, pl.ds(n, 1)], axis=1, keepdims=True)
        first[pl.ds(n, 1)] = column_to_row(column, eye)
        turned[n] = block.T
        return 0

    for c in range(n_chunks):
        fetch(c).wait()
        lax.fori_loop(c * CHUNK, c * CHUNK + CHUNK, first_row, 0, unroll=8)
        store(c).start()
    base = gx * ROWS

    def picks(n):
        return [jnp.clip(columns[k, 0, n] - base, 0, ROWS - 1) for k in range(3)]

    def second_row(n, _):
        change = change_row(own_blocks(blocks, n), turned[n], first, picks(n))
        second[pl.ds(n, 1)] = 2.0 * first[pl.ds(n, 1)] - change
        return 0

    second[...] = jnp.zeros_like(second)
    for c in range(n_chunks):
        block_copy(c).wait()
        lax.fori_loop(max(c * CHUNK, 2), min(c * CHUNK + CHUNK, ROWS - 2), second_row, 0, unroll=True)

    def residual_row(n, _):
        column = change_row(own_blocks(blocks, n), None, second, picks(n))
        residual[pl.ds(n, 1)] = column_to_row(column, eye)
        return 0

    lax.fori_loop(4, ROWS - 4, residual_row, 0, unroll=8)
    residual[...] = rows[1] * (rows[0] - residual[...])

    def scatter(n, total):
        return scattered(total, residual[pl.ds(n, 1)], indices[pl.ds(n, 1)], low_block)

    total_out[...] = lax.fori_loop(4, ROWS - 4, scatter, jnp.zeros((16, BS), f32), unroll=8)
    first_out[...] = first[...]
    second_out[...] = second[...]
    for c in range(n_chunks):
        store(c).wait()


def edges_kernel(
    rhs, weights, aggregates, columns, fine, turned_hbm, first, second, total_in, before_hbm, after_hbm,
    shared, first_field, second_own,
    blocks, turned, halo, field, ends, indices, halo_columns, sems,
):
    gx = lax.axis_index("gx")
    low_block = lax.axis_index("gy") * 4 - 2
    eye = identity_mask()
    copies = []
    for side, source in ((0, before_hbm), (1, after_hbm)):
        top, near = side * (ROWS - 4), side * (ROWS - 8)
        for at, (src, dst) in enumerate((
            (source.at[pl.ds(SMALL + 16, 8)], halo_columns.at[side]),
            (source, halo.at[side]),
            (fine.at[pl.ds(3 * top, 12)], blocks.at[side]),
            (turned_hbm.at[pl.ds(side * (ROWS - 2), 2)], turned.at[side]),
            (rhs.at[pl.ds(near, 8)], ends.at[side, 0]),
            (weights.at[pl.ds(near, 8)], ends.at[side, 1]),
            (aggregates.at[pl.ds(near, 8)], indices.at[side]),
        )):
            action = pltpu.make_async_copy(src, dst, sems.at[side, at])
            action.start()
            copies.append(action)
    base = gx * ROWS - 4
    first_field[4 : ROWS + 4] = first[...]
    field[4 : ROWS + 4] = second[...]
    field[0:2] = jnp.zeros((2, BS), f32)
    field[FEXT - 2 : FEXT] = jnp.zeros((2, BS), f32)
    for action in copies:
        action.wait()
    first_field[0:4] = halo[0, SMALL : SMALL + 4]
    first_field[FEXT - 4 : FEXT] = halo[1, SMALL : SMALL + 4]

    def edge_blocks(side, r):
        return [blocks[side, 3 * r + k] for k in range(3)]

    for side in range(2):
        for r in range(2):
            at = side * (ROWS + 2) + 2 + r
            change = halo_change(halo.at[side], r, first_field, halo_picks(halo_columns, side, r, base))
            field[at : at + 1] = 2.0 * first_field[at : at + 1] - change
            n = side * (ROWS - 2) + r
            change = change_row(
                edge_blocks(side, 2 * side + r), turned[side, r], first_field, picks_of(columns, n, base))
            field[n + 4 : n + 5] = 2.0 * first_field[n + 4 : n + 5] - change
    second_own[...] = field[4 : ROWS + 4]
    total = total_in[...]
    for side in range(2):
        for r in range(4):
            n, at = side * (ROWS - 4) + r, 4 * side + r
            column = change_row(edge_blocks(side, r), None, field, picks_of(columns, n, base))
            value = ends[side, 1, at : at + 1] * (ends[side, 0, at : at + 1] - column_to_row(column, eye))
            total = scattered(total, value, indices[side, at : at + 1], low_block)
    shared[0:8] = total[0:8] + total[8:16]
    shared[8:40] = jnp.zeros((32, BS), f32)
    shared[pl.ds(pl.multiple_of(8 + 8 * gx, 8), 8)] = jnp.concatenate(
        [field[4:8], field[FEXT - 8 : FEXT - 4]], axis=0)


def local_kernel(shared, mine, previous, following, out):
    eye = identity_mask()
    zero = jnp.zeros((1, BS), f32)
    own = [shared[j : j + 1] for j in range(8)]
    groups = (
        (previous, [zero, zero, own[0], own[1]]),
        (mine, own[2:6]),
        (following, [own[6], own[7], zero, zero]),
    )
    inner = [[right[0]] for _, right in groups]
    for j in range(1, 4):
        for (source, right), found in zip(groups, inner):
            found.append(right[j] - times_row(source[LOWER + j], found[-1], eye))
    solved = [[None] * 4 for _ in groups]
    for j in (3, 2, 1, 0):
        held = []
        for (source, _), found, x in zip(groups, inner, solved):
            held.append(found[j] if j == 3 else found[j] - times_row(source[UPPER + j], x[j + 1], eye))
        for (source, _), value, x in zip(groups, held, solved):
            x[j] = times_row(source[PIVOT + j], value, eye)
    tiles = []
    for found, x in zip(inner, solved):
        tiles += x + [found[3], zero, zero, zero]
    tile = jnp.concatenate(tiles, axis=0)
    for peer in range(GROUPS):
        out[peer] = tile


def correct_kernel(
    parts_hbm, shared, first_field, second_own, weights, aggregates, columns, maps, mine, previous, following,
    fine, turned_hbm, before_hbm, after_hbm,
    field_out, coarse_out,
    parts, chain, inside, blocks, turned, halo, sums, entering, leaving, window, field, next_field, halo_columns,
    weight_rows, indices, sems, chain_sems, block_sems,
):
    gx = lax.axis_index("gx")
    gy = lax.axis_index("gy")
    eye = identity_mask()
    step = 8
    chain_copies = {}
    arrived = pltpu.make_async_copy(parts_hbm, parts, sems.at[4])
    arrived.start()
    n_steps = GROUPS // step
    for kind, c in [(k, c) for c in range(n_steps) for k in (0, 1)] + [(2, c) for c in reversed(range(n_steps))]:
        action = pltpu.make_async_copy(
            maps.at[pl.ds(c * step, step), kind], chain.at[kind, pl.ds(c * step, step)], chain_sems.at[kind, c])
        action.start()
        chain_copies[kind, c] = action
    copies = [
        pltpu.make_async_copy(previous.at[pl.ds(INSIDE + 4, 4)], inside.at[pl.ds(0, 4)], sems.at[5]),
        pltpu.make_async_copy(mine.at[pl.ds(INSIDE, 8)], inside.at[pl.ds(4, 8)], sems.at[6]),
        pltpu.make_async_copy(following.at[pl.ds(INSIDE, 4)], inside.at[pl.ds(12, 4)], sems.at[7]),
        pltpu.make_async_copy(before_hbm.at[pl.ds(SMALL + 16, 8)], halo_columns.at[0], sems.at[0]),
        pltpu.make_async_copy(after_hbm.at[pl.ds(SMALL + 16, 8)], halo_columns.at[1], sems.at[1]),
        pltpu.make_async_copy(weights, weight_rows, sems.at[2]),
        pltpu.make_async_copy(aggregates, indices, sems.at[3]),
        pltpu.make_async_copy(before_hbm, halo.at[0], sems.at[8]),
        pltpu.make_async_copy(after_hbm, halo.at[1], sems.at[9]),
    ]
    whole = [pltpu.make_async_copy(turned_hbm, turned, sems.at[10])]
    for c in range(4):
        rows = pl.ds(c * (ROWS * 3 // 4), ROWS * 3 // 4)
        whole.append(pltpu.make_async_copy(fine.at[rows], blocks.at[rows], block_sems.at[c]))
    for action in copies + whole:
        action.start()
    before, after = halo.at[0], halo.at[1]
    arrived.wait()

    for d in range(GROUPS):
        total = parts[d, 8:16]
        if d + 1 < GROUPS:
            total += parts[d + 1, 0:8]
        if d > 0:
            total += parts[d - 1, 16:24]
        sums[d + 1] = total
    sums[0] = jnp.zeros((8, BS), f32)
    sums[GROUPS + 1] = jnp.zeros((8, BS), f32)

    entering[0:8] = jnp.zeros((8, BS), f32)
    value = jnp.zeros((1, BS), f32)
    heights = []
    for d in range(GROUPS):
        if d % step == 0:
            for kind in (0, 1):
                chain_copies[kind, d // step].wait()
        own, local = sums[d + 1, 4:5], sums[d + 1, 0:1]
        if d % 2 == 0:
            height = jnp.sum(chain[1, d] * value + jnp.where(eye, local, 0.0), axis=1, keepdims=True)
            value = jnp.sum(chain[0, d] * value + jnp.where(eye, own, 0.0), axis=1, keepdims=True)
            entering[d + 1 : d + 2] = column_to_row(value, eye)
        else:
            height = jnp.sum(chain[1, d] * value, axis=0, keepdims=True) + local
            value = jnp.sum(chain[0, d] * value, axis=0, keepdims=True) + own
            entering[d + 1 : d + 2] = value
        heights.append(column_to_row(height, eye) if d % 2 == 0 else height)
    leaving[GROUPS : GROUPS + 8] = jnp.zeros((8, BS), f32)
    value = None
    for d in reversed(range(GROUPS)):
        if d % step == step - 1:
            chain_copies[2, d // step].wait()
        if d == GROUPS - 1:
            value = heights[d]
        elif d % 2 == 0:
            value = jnp.sum(chain[2, d] * value + jnp.where(eye, heights[d], 0.0), axis=1, keepdims=True)
        else:
            value = jnp.sum(chain[2, d] * value, axis=0, keepdims=True) + heights[d]
        leaving[d : d + 1] = column_to_row(value, eye) if d % 2 == 0 else value

    for action in copies[:3]:
        action.wait()
    for j in range(8):
        offset, block = ((-1, j + 2), (0, j - 2), (1, j - 6))[(j + 2) // 4]
        group = gy + offset
        enter = entering[pl.ds(jnp.maximum(group, 0), 1)]
        leave = leaving[pl.ds(jnp.minimum(group + 1, GROUPS), 1)]
        total = inside[2 * j] * enter + inside[2 * j + 1] * leave
        window[j : j + 1] = column_to_row(jnp.sum(total, axis=1, keepdims=True), eye) + sums[
            group + 1, block : block + 1]
    coarse_out[...] = window[2:6]

    for action in copies[3:]:
        action.wait()
    low_block = gy * 4 - 2
    field[4 : ROWS + 4] = second_own[...]
    left = pl.multiple_of(8 + 8 * jnp.maximum(gx - 1, 0), 8)
    right = pl.multiple_of(8 + 8 * jnp.minimum(gx + 1, 3), 8)
    field[0:4] = shared[pl.ds(left, 8)][4:8]
    field[FEXT - 4 : FEXT] = shared[pl.ds(right, 8)][0:4]

    def interpolate(index, weight):
        block, within = (index >> 7) - low_block, index & 127
        total = jnp.zeros(index.shape, f32)
        for j in range(8):
            source = jnp.broadcast_to(window[j : j + 1], index.shape)
            total = jnp.where(block == j, jnp.take_along_axis(source, within, axis=1), total)
        return weight * total

    for at in range(ROWS // 8):
        rows = pl.ds(8 * at, 8)
        field[pl.ds(8 * at + 4, 8)] += interpolate(indices[rows], weight_rows[rows])
    for top, source in ((0, before), (FEXT - 4, after)):
        index = source[SMALL + 8 : SMALL + 16].astype(jnp.int32)
        weight = jnp.concatenate([source[SMALL + 4 : SMALL + 8], jnp.zeros((4, BS), f32)], axis=0)
        field[top : top + 4] += interpolate(index, weight)[0:4]

    base = gx * ROWS - 4
    next_field[0:2] = jnp.zeros((2, BS), f32)
    next_field[FEXT - 2 : FEXT] = jnp.zeros((2, BS), f32)
    whole[0].wait()

    def third(n, _):
        change = change_row(own_blocks(blocks, n), turned[n], field, picks_of(columns, n, base))
        rows = pl.ds(n + 4, 1)
        next_field[rows] = field[rows] + first_field[rows] - change
        return 0

    for c in range(4):
        whole[1 + c].wait()
        lax.fori_loop(c * ROWS // 4, (c + 1) * ROWS // 4, third, 0, unroll=8)
    for side, source in ((0, before), (1, after)):
        for r in range(2):
            at = side * (ROWS + 2) + 2 + r
            change = halo_change(source, r, field, halo_picks(halo_columns, side, r, base))
            next_field[at : at + 1] = field[at : at + 1] + first_field[at : at + 1] - change

    def fourth(n, _):
        change = change_row(own_blocks(blocks, n), turned[n], next_field, picks_of(columns, n, base))
        rows = pl.ds(n + 4, 1)
        field_out[pl.ds(n, 1)] = next_field[rows] + first_field[rows] - change
        return 0

    lax.fori_loop(0, ROWS, fourth, 0, unroll=8)


def per_device(
    rhs, fine_blocks, smoother, columns, aggregates, weights, coarse_lower, coarse_upper, coarse_pivot
):
    rhs, aggregates, weights, columns, smoother = rhs[0], aggregates[0], weights[0], columns.transpose(2, 0, 1), smoother[0]
    fine = fine_blocks.reshape(ROWS * 3, BS, BS)
    dma = pltpu.SemaphoreType.DMA

    maps, mine = pl.pallas_call(
        maps_kernel,
        name="maps",
        out_shape=(shape(3, BS, BS), shape(20, BS, BS)),
        in_specs=[HBM] * 3,
        out_specs=(HBM, HBM),
        scratch_shapes=[pltpu.VMEM((3, BS, BS), f32), pltpu.VMEM((20, BS, BS), f32), dma((3,)), dma((2,))],
        compiler_params=grant(58),
    )(coarse_lower, coarse_upper, coarse_pivot)
    gathered = lax.all_gather(maps, "gy", axis=0)

    to_previous, to_next, mine = pl.pallas_call(
        pack_kernel,
        name="pack",
        out_shape=(shape(HALO, BS), shape(HALO, BS), shape(20, BS, BS)),
        in_specs=[HBM] * 3 + [SMEM] + [HBM] * 3,
        out_specs=(HBM, HBM, HBM),
        scratch_shapes=[
            pltpu.VMEM((2, HALO, BS), f32), pltpu.VMEM((2, 4, BS, BS), f32), pltpu.VMEM((2, 2, 8, BS), f32),
            pltpu.VMEM((2, 8, BS), jnp.int32), dma((2, 5)), dma((2,)),
        ],
        input_output_aliases={6: 2},
        compiler_params=grant(58),
    )(rhs, weights, aggregates, columns, fine_blocks.reshape(ROWS * 3 * BS, BS), smoother, mine)
    before = lax.ppermute(to_next, "gx", [(i, i + 1) for i in range(3)])
    after = lax.ppermute(to_previous, "gx", [(i + 1, i) for i in range(3)])

    turned, first, second, total = pl.pallas_call(
        interior_kernel,
        name="interior",
        out_shape=(shape(ROWS, BS, BS), shape(ROWS, BS), shape(ROWS, BS), shape(16, BS)),
        in_specs=[HBM] * 3 + [SMEM] + [HBM] * 3,
        out_specs=(HBM, VMEM, VMEM, VMEM),
        scratch_shapes=[
            pltpu.VMEM((ROWS * 3, BS, BS), f32), pltpu.VMEM((ROWS, BS, BS), f32), pltpu.VMEM((ROWS, BS, BS), f32),
            pltpu.VMEM((ROWS, BS), f32), pltpu.VMEM((ROWS, BS), f32), pltpu.VMEM((ROWS, BS), f32),
            pltpu.VMEM((2, ROWS, BS), f32), pltpu.VMEM((ROWS, BS), jnp.int32),
            dma((2, ROWS // CHUNK)), dma((3,)), dma((ROWS // CHUNK,)),
        ],
        compiler_params=grant(58),
    )(rhs, weights, aggregates, columns, fine, smoother, to_next)

    shared, first_field, second_own = pl.pallas_call(
        edges_kernel,
        name="edges",
        out_shape=(shape(40, BS), shape(FEXT, BS), shape(ROWS, BS)),
        in_specs=[HBM] * 3 + [SMEM] + [HBM] * 2 + [VMEM] * 3 + [HBM] * 2,
        out_specs=(VMEM, VMEM, VMEM),
        scratch_shapes=[
            pltpu.VMEM((2, 12, BS, BS), f32), pltpu.VMEM((2, 2, BS, BS), f32), pltpu.VMEM((2, HALO, BS), f32),
            pltpu.VMEM((FEXT, BS), f32), pltpu.VMEM((2, 2, 8, BS), f32), pltpu.VMEM((2, 8, BS), jnp.int32),
            pltpu.SMEM((2, 8, BS), f32), dma((2, 7)),
        ],
        compiler_params=grant(58),
    )(rhs, weights, aggregates, columns, fine, turned, first, second, total, before, after)
    previous = lax.ppermute(mine, "gy", [(i, i + 1) for i in range(GROUPS - 1)])
    following = lax.ppermute(mine, "gy", [(i + 1, i) for i in range(GROUPS - 1)])
    for bit in (1, 2):
        shared = shared + lax.ppermute(shared, "gx", [(i, i ^ bit) for i in range(4)])

    spread = pl.pallas_call(
        local_kernel,
        name="local_solutions",
        out_shape=shape(GROUPS, 24, BS),
        in_specs=[VMEM] * 4,
        out_specs=VMEM,
        compiler_params=grant(40),
    )(shared, mine, previous, following)
    parts = lax.all_to_all(spread, "gy", 0, 0)

    field, coarse = pl.pallas_call(
        correct_kernel,
        name="correct",
        out_shape=(shape(ROWS, BS), shape(4, BS)),
        in_specs=[HBM] + [VMEM] * 3 + [HBM] * 2 + [SMEM] + [HBM] * 8,
        out_specs=(VMEM, VMEM),
        scratch_shapes=[
            pltpu.VMEM((GROUPS, 24, BS), f32), pltpu.VMEM((3, GROUPS, BS, BS), f32), pltpu.VMEM((16, BS, BS), f32),
            pltpu.VMEM((ROWS * 3, BS, BS), f32), pltpu.VMEM((ROWS, BS, BS), f32), pltpu.VMEM((2, HALO, BS), f32),
            pltpu.VMEM((GROUPS + 2, 8, BS), f32),
            pltpu.VMEM((GROUPS + 8, BS), f32), pltpu.VMEM((GROUPS + 8, BS), f32), pltpu.VMEM((8, BS), f32),
            pltpu.VMEM((FEXT, BS), f32), pltpu.VMEM((FEXT, BS), f32), pltpu.SMEM((2, 8, BS), f32),
            pltpu.VMEM((ROWS, BS), f32), pltpu.VMEM((ROWS, BS), jnp.int32), dma((11,)), dma((3, 4)), dma((4,)),
        ],
        compiler_params=grant(58),
    )(
        parts, shared, first_field, second_own, weights, aggregates, columns, gathered, mine, previous, following,
        fine, turned, before, after,
    )
    return (field[None], coarse)


def solution(mesh):
    return jax.shard_map(
        per_device,
        mesh=mesh,
        in_specs=(
            P("gy", "gx", None),
            P("gy", "gx", None, None, None),
            P("gy", "gx", None, None),
            P("gy", "gx", None),
            P("gy", "gx", None),
            P("gy", "gx", None),
            P("gy", None, None),
            P("gy", None, None),
            P("gy", None, None),
        ),
        out_specs=(P("gy", "gx", None), P("gy", None)),
        check_vma=False,
    )
```

```python
import jax
import jax.numpy as jnp
from jax import lax
from jax.experimental import pallas as pl
from jax.experimental.pallas import tpu as pltpu
from jax.sharding import PartitionSpec as P

BS = 128
ROWS = 64
FEXT = ROWS + 8
CHUNK = 8
LOWER, UPPER, PIVOT, MINE, FOR_PREVIOUS, FOR_NEXT = 3, 7, 10, 18, 14, 12
GROUPS = 32
TURNED, SMALL, HALO = 768, 1024, 1048
f32 = jnp.float32
VMEM = pl.BlockSpec(memory_space=pltpu.VMEM)
SMEM = pl.BlockSpec(memory_space=pltpu.SMEM)
HBM = pl.BlockSpec(memory_space=pltpu.HBM)


def grant(mib):
    return pltpu.CompilerParams(vmem_limit_bytes=mib * 1024 * 1024)


def shape(*dims):
    return jax.ShapeDtypeStruct(dims, f32)


def identity_mask():
    rows = lax.broadcasted_iota(jnp.int32, (BS, BS), 0)
    columns = lax.broadcasted_iota(jnp.int32, (BS, BS), 1)
    return rows == columns


def column_to_row(column, eye):
    return jnp.sum(jnp.where(eye, column, 0.0), axis=0, keepdims=True)


def times_row(matrix, row, eye):
    return column_to_row(jnp.sum(matrix * row, axis=1, keepdims=True), eye)


def halves(value):
    high = value.astype(jnp.bfloat16)
    return high, (value - high.astype(f32)).astype(jnp.bfloat16)


def product(left, right):
    left_high, left_low = halves(left)
    right_high, right_low = halves(right)
    return jnp.dot(
        jnp.concatenate([left_high, left_high, left_low], axis=1),
        jnp.concatenate([right_high, right_low, right_high], axis=0),
        preferred_element_type=f32,
    )


def inside_at(j):
    return 2 * j if j < 2 else 10 + 2 * j


def prepare_kernel(
    lower, upper, pivot, rhs, weights, aggregates, columns, fine, smoother,
    maps_out, mine_out, for_previous, for_next, to_previous, to_next,
    maps, mine, spare, packed, edge, ends, indices, coarse_sems, sems, out_sems,
):
    eye = identity_mask()
    parts = (
        (lower.at[pl.ds(0, 1)], spare.at[pl.ds(0, 1)]),
        (lower.at[pl.ds(1, 3)], mine.at[pl.ds(LOWER + 1, 3)]),
        (pivot, mine.at[pl.ds(PIVOT, 4)]),
        (upper.at[pl.ds(3, 1)], spare.at[pl.ds(1, 1)]),
        (upper.at[pl.ds(0, 3)], mine.at[pl.ds(UPPER, 3)]),
    )
    coarse = [pltpu.make_async_copy(src, dst, coarse_sems.at[at]) for at, (src, dst) in enumerate(parts)]
    for action in coarse:
        action.start()

    def start(source, target, *at):
        action = pltpu.make_async_copy(source, target, sems.at[at])
        action.start()
        return action

    near, far = [], []
    for side in range(2):
        top = side * (ROWS - 8)
        near.append(start(smoother.at[pl.ds(side * (ROWS - 4), 4)], edge.at[side], side, 0))
        near.append(start(rhs.at[pl.ds(top, 8)], ends.at[side, 0], side, 1))
        near.append(start(weights.at[pl.ds(top, 8)], ends.at[side, 1], side, 2))
        near.append(start(aggregates.at[pl.ds(top, 8)], indices.at[side], side, 3))
    for side in range(2):
        far.append(start(fine.at[pl.ds(side * (ROWS - 2) * 3 * BS, TURNED)], packed.at[side, pl.ds(0, TURNED)], side, 4))
    for action in coarse + near:
        action.wait()
    lane = lax.broadcasted_iota(jnp.int32, (8, BS), 1)
    for side in range(2):
        top = 4 * side
        packed[side, TURNED : TURNED + BS] = edge[side, 2 * side].T
        packed[side, TURNED + BS : SMALL] = edge[side, 2 * side + 1].T
        for r in range(4):
            packed[side, SMALL + r : SMALL + r + 1] = times_row(
                edge[side, r], ends[side, 0, top + r : top + r + 1], eye)
        packed[side, SMALL + 4 : SMALL + 8] = ends[side, 1, top : top + 4]
        packed[side, SMALL + 8 : SMALL + 12] = indices[side, top : top + 4].astype(f32)
        packed[side, SMALL + 12 : SMALL + 16] = jnp.zeros((4, BS), f32)
        picked = jnp.zeros((8, BS), jnp.int32)
        for r in range(2):
            for k in range(3):
                picked = jnp.where(lane == 3 * r + k, columns[k, 0, side * (ROWS - 2) + r], picked)
        packed[side, SMALL + 16 : HALO] = picked.astype(f32)
    forward = [-spare[0]]
    for j in range(1, 4):
        forward.append(-product(mine[LOWER + j], forward[-1]))
    both = product(mine[PIVOT + 3], jnp.concatenate([forward[3], -spare[1]], axis=1))
    for j in (3, 2, 1, 0):
        if j < 3:
            both = product(mine[UPPER + j], both)
            both = product(mine[PIVOT + j], jnp.concatenate([forward[j] - both[:, :BS], -both[:, BS:]], axis=1))
        mine[inside_at(j)] = both[:, :BS]
        mine[inside_at(j) + 1] = both[:, BS:]
    odd = lax.axis_index("gy") % 2 == 1
    for at, value in enumerate((forward[3], both[:, :BS], both[:, BS:])):
        maps[at] = jnp.where(odd, value.T, value)
    for action in far:
        action.wait()
    sent = [
        pltpu.make_async_copy(packed.at[0], to_previous, out_sems.at[4]),
        pltpu.make_async_copy(packed.at[1], to_next, out_sems.at[5]),
        pltpu.make_async_copy(maps, maps_out, out_sems.at[0]),
        pltpu.make_async_copy(mine, mine_out, out_sems.at[1]),
        pltpu.make_async_copy(mine.at[pl.ds(0, FOR_PREVIOUS)], for_previous, out_sems.at[2]),
        pltpu.make_async_copy(mine.at[pl.ds(MINE - FOR_NEXT, FOR_NEXT)], for_next, out_sems.at[3]),
    ]
    for action in sent:
        action.start()
    for action in sent:
        action.wait()


def change_row(blocks, turned_block, source, picks):
    total = blocks[0] * source[pl.ds(picks[0], 1)]
    total += blocks[1] * source[pl.ds(picks[1], 1)]
    total += blocks[2] * source[pl.ds(picks[2], 1)]
    column = jnp.sum(total, axis=1, keepdims=True)
    if turned_block is None:
        return column
    return jnp.sum(turned_block * column, axis=0, keepdims=True)


def own_blocks(blocks, n):
    return [blocks[3 * n + k] for k in range(3)]


def halo_change(halo, r, source, picks):
    blocks = [halo[(3 * r + k) * BS : (3 * r + k + 1) * BS] for k in range(3)]
    return change_row(blocks, halo[TURNED + r * BS : TURNED + (r + 1) * BS], source, picks)


def picks_of(columns, n, base):
    return [jnp.clip(columns[k, 0, n] - base, 0, FEXT - 1) for k in range(3)]


def halo_picks(halo_columns, side, r, base):
    return [
        jnp.clip(halo_columns[side, 0, 3 * r + k].astype(jnp.int32) - base, 0, FEXT - 1) for k in range(3)]


def scattered(total, value, index, low_block):
    row8 = lax.broadcasted_iota(jnp.int32, (8, BS), 0)
    row128 = lax.broadcasted_iota(jnp.int32, (BS, BS), 0)
    block, within = (index >> 7) - low_block, index & 127
    value = jnp.where(row8 == block, value, 0.0)
    high = value.astype(jnp.bfloat16).astype(f32)
    parts = jnp.concatenate([high, value - high], axis=0).astype(jnp.bfloat16)
    hot = jnp.where(row128 == within, 1.0, 0.0).astype(jnp.bfloat16)
    return total + lax.dot_general(parts, hot, (((1,), (1,)), ((), ())), preferred_element_type=f32)


def interior_kernel(
    rhs, weights, aggregates, columns, fine, smoother, packed,
    turned_out, first_out, second_out, total_out,
    blocks, smooth, turned, first, second, residual, rows, indices, sems, small_sems, out_sems,
):
    gx = lax.axis_index("gx")
    low_block = lax.axis_index("gy") * 4 - 2
    eye = identity_mask()
    n_chunks = ROWS // CHUNK
    small = [
        pltpu.make_async_copy(rhs, rows.at[0], small_sems.at[0]),
        pltpu.make_async_copy(weights, rows.at[1], small_sems.at[1]),
        pltpu.make_async_copy(aggregates, indices, small_sems.at[2]),
    ]
    for action in small:
        action.start()

    def fetch(c):
        part = pl.ds(c * CHUNK, CHUNK)
        return pltpu.make_async_copy(smoother.at[part], smooth.at[part], sems.at[0, c])

    def block_copy(c):
        part = pl.ds(c * CHUNK * 3, CHUNK * 3)
        return pltpu.make_async_copy(fine.at[part], blocks.at[part], sems.at[1, c])

    def store(c):
        part = pl.ds(c * CHUNK, CHUNK)
        return pltpu.make_async_copy(turned.at[part], turned_out.at[part], out_sems.at[c])

    for c in range(n_chunks):
        fetch(c).start()
    for c in range(n_chunks):
        block_copy(c).start()
    for action in small:
        action.wait()

    def first_row(n, _):
        block = smooth[n]
        column = jnp.sum(block * rows[0, pl.ds(n, 1)], axis=1, keepdims=True)
        first[pl.ds(n, 1)] = column_to_row(column, eye)
        turned[n] = block.T
        return 0

    for c in range(n_chunks):
        fetch(c).wait()
        lax.fori_loop(c * CHUNK, c * CHUNK + CHUNK, first_row, 0, unroll=8)
        store(c).start()
    base = gx * ROWS

    def picks(n):
        return [jnp.clip(columns[k, 0, n] - base, 0, ROWS - 1) for k in range(3)]

    def second_row(n, _):
        change = change_row(own_blocks(blocks, n), turned[n], first, picks(n))
        second[pl.ds(n, 1)] = 2.0 * first[pl.ds(n, 1)] - change
        return 0

    second[...] = jnp.zeros_like(second)
    for c in range(n_chunks):
        block_copy(c).wait()
        lax.fori_loop(max(c * CHUNK, 2), min(c * CHUNK + CHUNK, ROWS - 2), second_row, 0, unroll=True)

    def residual_row(n, _):
        column = change_row(own_blocks(blocks, n), None, second, picks(n))
        residual[pl.ds(n, 1)] = column_to_row(column, eye)
        return 0

    lax.fori_loop(4, ROWS - 4, residual_row, 0, unroll=8)
    residual[...] = rows[1] * (rows[0] - residual[...])

    def scatter(n, total):
        return scattered(total, residual[pl.ds(n, 1)], indices[pl.ds(n, 1)], low_block)

    total_out[...] = lax.fori_loop(4, ROWS - 4, scatter, jnp.zeros((16, BS), f32), unroll=8)
    first_out[...] = first[...]
    second_out[...] = second[...]
    for c in range(n_chunks):
        store(c).wait()


def edges_kernel(
    rhs, weights, aggregates, columns, fine, turned_hbm, first, second, total_in, before, after,
    shared, first_field, second_own,
    blocks, turned, field, ends, indices, halo_columns, sems,
):
    gx = lax.axis_index("gx")
    low_block = lax.axis_index("gy") * 4 - 2
    eye = identity_mask()
    copies = []
    halo = (before, after)
    for side, source in enumerate(halo):
        top, near = side * (ROWS - 4), side * (ROWS - 8)
        for at, (src, dst) in enumerate((
            (source.at[pl.ds(SMALL + 16, 8)], halo_columns.at[side]),
            (fine.at[pl.ds(3 * top, 12)], blocks.at[side]),
            (turned_hbm.at[pl.ds(side * (ROWS - 2), 2)], turned.at[side]),
            (rhs.at[pl.ds(near, 8)], ends.at[side, 0]),
            (weights.at[pl.ds(near, 8)], ends.at[side, 1]),
            (aggregates.at[pl.ds(near, 8)], indices.at[side]),
        )):
            action = pltpu.make_async_copy(src, dst, sems.at[side, at])
            action.start()
            copies.append(action)
    base = gx * ROWS - 4
    first_field[4 : ROWS + 4] = first[...]
    field[4 : ROWS + 4] = second[...]
    field[0:2] = jnp.zeros((2, BS), f32)
    field[FEXT - 2 : FEXT] = jnp.zeros((2, BS), f32)
    for action in copies:
        action.wait()
    first_field[0:4] = before[SMALL : SMALL + 4]
    first_field[FEXT - 4 : FEXT] = after[SMALL : SMALL + 4]

    def edge_blocks(side, r):
        return [blocks[side, 3 * r + k] for k in range(3)]

    for side in range(2):
        for r in range(2):
            at = side * (ROWS + 2) + 2 + r
            change = halo_change(halo[side], r, first_field, halo_picks(halo_columns, side, r, base))
            field[at : at + 1] = 2.0 * first_field[at : at + 1] - change
            n = side * (ROWS - 2) + r
            change = change_row(
                edge_blocks(side, 2 * side + r), turned[side, r], first_field, picks_of(columns, n, base))
            field[n + 4 : n + 5] = 2.0 * first_field[n + 4 : n + 5] - change
    second_own[...] = field[4 : ROWS + 4]
    total = total_in[...]
    for side in range(2):
        for r in range(4):
            n, at = side * (ROWS - 4) + r, 4 * side + r
            column = change_row(edge_blocks(side, r), None, field, picks_of(columns, n, base))
            value = ends[side, 1, at : at + 1] * (ends[side, 0, at : at + 1] - column_to_row(column, eye))
            total = scattered(total, value, indices[side, at : at + 1], low_block)
    shared[0:8] = total[0:8] + total[8:16]
    shared[8:40] = jnp.zeros((32, BS), f32)
    shared[pl.ds(pl.multiple_of(8 + 8 * gx, 8), 8)] = jnp.concatenate(
        [field[4:8], field[FEXT - 8 : FEXT - 4]], axis=0)


def local_kernel(shared, mine, previous, following, out):
    eye = identity_mask()
    zero = jnp.zeros((1, BS), f32)
    own = [shared[j : j + 1] for j in range(8)]
    groups = (
        (previous, MINE - FOR_NEXT, [zero, zero, own[0], own[1]]),
        (mine, 0, own[2:6]),
        (following, 0, [own[6], own[7], zero, zero]),
    )
    inner = [[right[0]] for _, _, right in groups]
    for j in range(1, 4):
        for at, ((source, start, right), found) in enumerate(zip(groups, inner)):
            if at == 0 and j < 3:
                found.append(right[j])
            else:
                found.append(right[j] - times_row(source[LOWER + j - start], found[-1], eye))
    solved = [[None] * 4 for _ in groups]
    for j in (3, 2, 1, 0):
        held = []
        for (source, start, _), found, x in zip(groups, inner, solved):
            held.append(
                found[j] if j == 3 else found[j] - times_row(source[UPPER + j - start], x[j + 1], eye))
        for (source, start, _), value, x in zip(groups, held, solved):
            x[j] = times_row(source[PIVOT + j - start], value, eye)
    tiles = []
    for found, x in zip(inner, solved):
        tiles += x + [found[3], zero, zero, zero]
    tile = jnp.concatenate(tiles, axis=0)
    for peer in range(GROUPS):
        out[peer] = tile


def correct_kernel(
    parts_hbm, shared, first_field, second_own, weights, aggregates, columns, maps, mine, previous, following,
    fine, turned_hbm, before_hbm, after_hbm,
    field_out, coarse_out,
    parts, chain, inside, blocks, turned, halo, sums, entering, leaving, window, field, next_field, halo_columns,
    weight_rows, indices, sems, chain_sems, block_sems,
):
    gx = lax.axis_index("gx")
    gy = lax.axis_index("gy")
    eye = identity_mask()
    step = 8
    chain_copies = {}
    arrived = pltpu.make_async_copy(parts_hbm, parts, sems.at[4])
    arrived.start()
    n_steps = GROUPS // step
    for kind, c in [(k, c) for c in range(n_steps) for k in (0, 1)] + [(2, c) for c in reversed(range(n_steps))]:
        action = pltpu.make_async_copy(
            maps.at[pl.ds(c * step, step), kind], chain.at[kind, pl.ds(c * step, step)], chain_sems.at[kind, c])
        action.start()
        chain_copies[kind, c] = action
    copies = [
        pltpu.make_async_copy(previous.at[pl.ds(FOR_NEXT - 4, 4)], inside.at[pl.ds(0, 4)], sems.at[5]),
        pltpu.make_async_copy(mine.at[pl.ds(0, 4)], inside.at[pl.ds(4, 4)], sems.at[6]),
        pltpu.make_async_copy(mine.at[pl.ds(MINE - 4, 4)], inside.at[pl.ds(8, 4)], sems.at[11]),
        pltpu.make_async_copy(following.at[pl.ds(0, 4)], inside.at[pl.ds(12, 4)], sems.at[7]),
        pltpu.make_async_copy(before_hbm.at[pl.ds(SMALL + 16, 8)], halo_columns.at[0], sems.at[0]),
        pltpu.make_async_copy(after_hbm.at[pl.ds(SMALL + 16, 8)], halo_columns.at[1], sems.at[1]),
        pltpu.make_async_copy(weights, weight_rows, sems.at[2]),
        pltpu.make_async_copy(aggregates, indices, sems.at[3]),
        pltpu.make_async_copy(before_hbm, halo.at[0], sems.at[8]),
        pltpu.make_async_copy(after_hbm, halo.at[1], sems.at[9]),
    ]
    whole = [pltpu.make_async_copy(turned_hbm, turned, sems.at[10])]
    for c in range(4):
        rows = pl.ds(c * (ROWS * 3 // 4), ROWS * 3 // 4)
        whole.append(pltpu.make_async_copy(fine.at[rows], blocks.at[rows], block_sems.at[c]))
    for action in copies + whole:
        action.start()
    before, after = halo.at[0], halo.at[1]
    arrived.wait()

    for d in range(GROUPS):
        total = parts[d, 8:16]
        if d + 1 < GROUPS:
            total += parts[d + 1, 0:8]
        if d > 0:
            total += parts[d - 1, 16:24]
        sums[d + 1] = total
    sums[0] = jnp.zeros((8, BS), f32)
    sums[GROUPS + 1] = jnp.zeros((8, BS), f32)

    entering[0:8] = jnp.zeros((8, BS), f32)
    value = jnp.zeros((1, BS), f32)
    heights = []
    for d in range(GROUPS):
        if d % step == 0:
            for kind in (0, 1):
                chain_copies[kind, d // step].wait()
        own, local = sums[d + 1, 4:5], sums[d + 1, 0:1]
        if d % 2 == 0:
            height = jnp.sum(chain[1, d] * value + jnp.where(eye, local, 0.0), axis=1, keepdims=True)
            value = jnp.sum(chain[0, d] * value + jnp.where(eye, own, 0.0), axis=1, keepdims=True)
            entering[d + 1 : d + 2] = column_to_row(value, eye)
        else:
            height = jnp.sum(chain[1, d] * value, axis=0, keepdims=True) + local
            value = jnp.sum(chain[0, d] * value, axis=0, keepdims=True) + own
            entering[d + 1 : d + 2] = value
        heights.append(column_to_row(height, eye) if d % 2 == 0 else height)
    leaving[GROUPS : GROUPS + 8] = jnp.zeros((8, BS), f32)
    value = None
    for d in reversed(range(GROUPS)):
        if d % step == step - 1:
            chain_copies[2, d // step].wait()
        if d == GROUPS - 1:
            value = heights[d]
        elif d % 2 == 0:
            value = jnp.sum(chain[2, d] * value + jnp.where(eye, heights[d], 0.0), axis=1, keepdims=True)
        else:
            value = jnp.sum(chain[2, d] * value, axis=0, keepdims=True) + heights[d]
        leaving[d : d + 1] = column_to_row(value, eye) if d % 2 == 0 else value

    for action in copies[:4]:
        action.wait()
    for j in range(8):
        offset, block = ((-1, j + 2), (0, j - 2), (1, j - 6))[(j + 2) // 4]
        group = gy + offset
        enter = entering[pl.ds(jnp.maximum(group, 0), 1)]
        leave = leaving[pl.ds(jnp.minimum(group + 1, GROUPS), 1)]
        total = inside[2 * j] * enter + inside[2 * j + 1] * leave
        window[j : j + 1] = column_to_row(jnp.sum(total, axis=1, keepdims=True), eye) + sums[
            group + 1, block : block + 1]
    coarse_out[...] = window[2:6]

    for action in copies[4:]:
        action.wait()
    low_block = gy * 4 - 2
    field[4 : ROWS + 4] = second_own[...]
    left = pl.multiple_of(8 + 8 * jnp.maximum(gx - 1, 0), 8)
    right = pl.multiple_of(8 + 8 * jnp.minimum(gx + 1, 3), 8)
    field[0:4] = shared[pl.ds(left, 8)][4:8]
    field[FEXT - 4 : FEXT] = shared[pl.ds(right, 8)][0:4]

    def interpolate(index, weight):
        block, within = (index >> 7) - low_block, index & 127
        total = jnp.zeros(index.shape, f32)
        for j in range(8):
            source = jnp.broadcast_to(window[j : j + 1], index.shape)
            total = jnp.where(block == j, jnp.take_along_axis(source, within, axis=1), total)
        return weight * total

    for at in range(ROWS // 8):
        rows = pl.ds(8 * at, 8)
        field[pl.ds(8 * at + 4, 8)] += interpolate(indices[rows], weight_rows[rows])
    for top, source in ((0, before), (FEXT - 4, after)):
        index = source[SMALL + 8 : SMALL + 16].astype(jnp.int32)
        weight = jnp.concatenate([source[SMALL + 4 : SMALL + 8], jnp.zeros((4, BS), f32)], axis=0)
        field[top : top + 4] += interpolate(index, weight)[0:4]

    base = gx * ROWS - 4
    next_field[0:2] = jnp.zeros((2, BS), f32)
    next_field[FEXT - 2 : FEXT] = jnp.zeros((2, BS), f32)
    whole[0].wait()

    def third(n, _):
        change = change_row(own_blocks(blocks, n), turned[n], field, picks_of(columns, n, base))
        rows = pl.ds(n + 4, 1)
        next_field[rows] = field[rows] + first_field[rows] - change
        return 0

    for c in range(4):
        whole[1 + c].wait()
        lax.fori_loop(c * ROWS // 4, (c + 1) * ROWS // 4, third, 0, unroll=8)
    for side, source in ((0, before), (1, after)):
        for r in range(2):
            at = side * (ROWS + 2) + 2 + r
            change = halo_change(source, r, field, halo_picks(halo_columns, side, r, base))
            next_field[at : at + 1] = field[at : at + 1] + first_field[at : at + 1] - change

    def fourth(n, _):
        change = change_row(own_blocks(blocks, n), turned[n], next_field, picks_of(columns, n, base))
        rows = pl.ds(n + 4, 1)
        field_out[pl.ds(n, 1)] = next_field[rows] + first_field[rows] - change
        return 0

    lax.fori_loop(0, ROWS, fourth, 0, unroll=8)


def per_device(
    rhs, fine_blocks, smoother, columns, aggregates, weights, coarse_lower, coarse_upper, coarse_pivot
):
    rhs, aggregates, weights, columns, smoother = rhs[0], aggregates[0], weights[0], columns.transpose(2, 0, 1), smoother[0]
    fine = fine_blocks.reshape(ROWS * 3, BS, BS)
    dma = pltpu.SemaphoreType.DMA

    maps, mine, for_previous, for_next, to_previous, to_next = pl.pallas_call(
        prepare_kernel,
        name="prepare",
        out_shape=(
            shape(3, BS, BS), shape(MINE, BS, BS), shape(FOR_PREVIOUS, BS, BS), shape(FOR_NEXT, BS, BS),
            shape(HALO, BS), shape(HALO, BS)),
        in_specs=[HBM] * 6 + [SMEM] + [HBM] * 2,
        out_specs=(HBM,) * 6,
        scratch_shapes=[
            pltpu.VMEM((3, BS, BS), f32), pltpu.VMEM((MINE, BS, BS), f32), pltpu.VMEM((2, BS, BS), f32),
            pltpu.VMEM((2, HALO, BS), f32), pltpu.VMEM((2, 4, BS, BS), f32), pltpu.VMEM((2, 2, 8, BS), f32),
            pltpu.VMEM((2, 8, BS), jnp.int32), dma((5,)), dma((2, 5)), dma((6,)),
        ],
        compiler_params=grant(58),
    )(
        coarse_lower, coarse_upper, coarse_pivot, rhs, weights, aggregates, columns,
        fine_blocks.reshape(ROWS * 3 * BS, BS), smoother,
    )
    gathered = lax.all_gather(maps, "gy", axis=0)

    before = lax.ppermute(to_next, "gx", [(i, i + 1) for i in range(3)])
    after = lax.ppermute(to_previous, "gx", [(i + 1, i) for i in range(3)])

    turned, first, second, total = pl.pallas_call(
        interior_kernel,
        name="interior",
        out_shape=(shape(ROWS, BS, BS), shape(ROWS, BS), shape(ROWS, BS), shape(16, BS)),
        in_specs=[HBM] * 3 + [SMEM] + [HBM] * 3,
        out_specs=(HBM, VMEM, VMEM, VMEM),
        scratch_shapes=[
            pltpu.VMEM((ROWS * 3, BS, BS), f32), pltpu.VMEM((ROWS, BS, BS), f32), pltpu.VMEM((ROWS, BS, BS), f32),
            pltpu.VMEM((ROWS, BS), f32), pltpu.VMEM((ROWS, BS), f32), pltpu.VMEM((ROWS, BS), f32),
            pltpu.VMEM((2, ROWS, BS), f32), pltpu.VMEM((ROWS, BS), jnp.int32),
            dma((2, ROWS // CHUNK)), dma((3,)), dma((ROWS // CHUNK,)),
        ],
        compiler_params=grant(58),
    )(rhs, weights, aggregates, columns, fine, smoother, to_next)

    shared, first_field, second_own = pl.pallas_call(
        edges_kernel,
        name="edges",
        out_shape=(shape(40, BS), shape(FEXT, BS), shape(ROWS, BS)),
        in_specs=[HBM] * 3 + [SMEM] + [HBM] * 2 + [VMEM] * 5,
        out_specs=(VMEM, VMEM, VMEM),
        scratch_shapes=[
            pltpu.VMEM((2, 12, BS, BS), f32), pltpu.VMEM((2, 2, BS, BS), f32),
            pltpu.VMEM((FEXT, BS), f32), pltpu.VMEM((2, 2, 8, BS), f32), pltpu.VMEM((2, 8, BS), jnp.int32),
            pltpu.SMEM((2, 8, BS), f32), dma((2, 6)),
        ],
        compiler_params=grant(54),
    )(rhs, weights, aggregates, columns, fine, turned, first, second, total, before, after)
    previous = lax.ppermute(for_next, "gy", [(i, i + 1) for i in range(GROUPS - 1)])
    following = lax.ppermute(for_previous, "gy", [(i + 1, i) for i in range(GROUPS - 1)])
    for bit in (1, 2):
        shared = shared + lax.ppermute(shared, "gx", [(i, i ^ bit) for i in range(4)])

    spread = pl.pallas_call(
        local_kernel,
        name="local_solutions",
        out_shape=shape(GROUPS, 24, BS),
        in_specs=[VMEM] * 4,
        out_specs=VMEM,
        compiler_params=grant(40),
    )(shared, mine, previous, following)
    parts = lax.all_to_all(spread, "gy", 0, 0)

    field, coarse = pl.pallas_call(
        correct_kernel,
        name="correct",
        out_shape=(shape(ROWS, BS), shape(4, BS)),
        in_specs=[HBM] + [VMEM] * 3 + [HBM] * 2 + [SMEM] + [HBM] * 8,
        out_specs=(VMEM, VMEM),
        scratch_shapes=[
            pltpu.VMEM((GROUPS, 24, BS), f32), pltpu.VMEM((3, GROUPS, BS, BS), f32), pltpu.VMEM((16, BS, BS), f32),
            pltpu.VMEM((ROWS * 3, BS, BS), f32), pltpu.VMEM((ROWS, BS, BS), f32), pltpu.VMEM((2, HALO, BS), f32),
            pltpu.VMEM((GROUPS + 2, 8, BS), f32),
            pltpu.VMEM((GROUPS + 8, BS), f32), pltpu.VMEM((GROUPS + 8, BS), f32), pltpu.VMEM((8, BS), f32),
            pltpu.VMEM((FEXT, BS), f32), pltpu.VMEM((FEXT, BS), f32), pltpu.SMEM((2, 8, BS), f32),
            pltpu.VMEM((ROWS, BS), f32), pltpu.VMEM((ROWS, BS), jnp.int32), dma((12,)), dma((3, 4)), dma((4,)),
        ],
        compiler_params=grant(58),
    )(
        parts, shared, first_field, second_own, weights, aggregates, columns, gathered, mine, previous, following,
        fine, turned, before, after,
    )
    return (field[None], coarse)


def solution(mesh):
    return jax.shard_map(
        per_device,
        mesh=mesh,
        in_specs=(
            P("gy", "gx", None),
            P("gy", "gx", None, None, None),
            P("gy", "gx", None, None),
            P("gy", "gx", None),
            P("gy", "gx", None),
            P("gy", "gx", None),
            P("gy", None, None),
            P("gy", None, None),
            P("gy", None, None),
        ),
        out_specs=(P("gy", "gx", None), P("gy", None)),
        check_vma=False,
    )
```

```python
import jax
import jax.numpy as jnp
from jax import lax
from jax.experimental import pallas as pl
from jax.experimental.pallas import tpu as pltpu
from jax.sharding import PartitionSpec as P

BS = 128
ROWS = 64
FEXT = ROWS + 8
CHUNK = 8
LOWER, UPPER, PIVOT, MINE, FOR_PREVIOUS, FOR_NEXT = 3, 7, 10, 18, 14, 12
GROUPS = 32
TURNED, SMALL, HALO = 768, 1024, 1048
f32 = jnp.float32
VMEM = pl.BlockSpec(memory_space=pltpu.VMEM)
SMEM = pl.BlockSpec(memory_space=pltpu.SMEM)
HBM = pl.BlockSpec(memory_space=pltpu.HBM)


def grant(mib):
    return pltpu.CompilerParams(vmem_limit_bytes=mib * 1024 * 1024)


def shape(*dims):
    return jax.ShapeDtypeStruct(dims, f32)


def identity_mask():
    rows = lax.broadcasted_iota(jnp.int32, (BS, BS), 0)
    columns = lax.broadcasted_iota(jnp.int32, (BS, BS), 1)
    return rows == columns


def column_to_row(column, eye):
    return jnp.sum(jnp.where(eye, column, 0.0), axis=0, keepdims=True)


def times_row(matrix, row, eye):
    return column_to_row(jnp.sum(matrix * row, axis=1, keepdims=True), eye)


def halves(value):
    high = value.astype(jnp.bfloat16)
    return high, (value - high.astype(f32)).astype(jnp.bfloat16)


def product(left, right):
    left_high, left_low = halves(left)
    right_high, right_low = halves(right)
    return jnp.dot(
        jnp.concatenate([left_high, left_high, left_low], axis=1),
        jnp.concatenate([right_high, right_low, right_high], axis=0),
        preferred_element_type=f32,
    )


def inside_at(j):
    return 2 * j if j < 2 else 10 + 2 * j


def prepare_kernel(
    lower, upper, pivot, rhs, weights, aggregates, columns, fine, smoother,
    maps_out, mine_out, for_previous, for_next, to_previous, to_next,
    maps, mine, spare, packed, edge, ends, indices, coarse_sems, sems, out_sems,
):
    eye = identity_mask()
    parts = (
        (lower.at[pl.ds(0, 1)], spare.at[pl.ds(0, 1)]),
        (lower.at[pl.ds(1, 3)], mine.at[pl.ds(LOWER + 1, 3)]),
        (pivot, mine.at[pl.ds(PIVOT, 4)]),
        (upper.at[pl.ds(3, 1)], spare.at[pl.ds(1, 1)]),
        (upper.at[pl.ds(0, 3)], mine.at[pl.ds(UPPER, 3)]),
    )
    coarse = [pltpu.make_async_copy(src, dst, coarse_sems.at[at]) for at, (src, dst) in enumerate(parts)]
    for action in coarse:
        action.start()

    def start(source, target, *at):
        action = pltpu.make_async_copy(source, target, sems.at[at])
        action.start()
        return action

    near, far = [], []
    for side in range(2):
        top = side * (ROWS - 8)
        near.append(start(smoother.at[pl.ds(side * (ROWS - 4), 4)], edge.at[side], side, 0))
        near.append(start(rhs.at[pl.ds(top, 8)], ends.at[side, 0], side, 1))
        near.append(start(weights.at[pl.ds(top, 8)], ends.at[side, 1], side, 2))
        near.append(start(aggregates.at[pl.ds(top, 8)], indices.at[side], side, 3))
    for side in range(2):
        far.append(start(fine.at[pl.ds(side * (ROWS - 2) * 3 * BS, TURNED)], packed.at[side, pl.ds(0, TURNED)], side, 4))
    for action in coarse + near:
        action.wait()
    lane = lax.broadcasted_iota(jnp.int32, (8, BS), 1)
    for side in range(2):
        top = 4 * side
        packed[side, TURNED : TURNED + BS] = edge[side, 2 * side].T
        packed[side, TURNED + BS : SMALL] = edge[side, 2 * side + 1].T
        for r in range(4):
            packed[side, SMALL + r : SMALL + r + 1] = times_row(
                edge[side, r], ends[side, 0, top + r : top + r + 1], eye)
        packed[side, SMALL + 4 : SMALL + 8] = ends[side, 1, top : top + 4]
        packed[side, SMALL + 8 : SMALL + 12] = indices[side, top : top + 4].astype(f32)
        packed[side, SMALL + 12 : SMALL + 16] = jnp.zeros((4, BS), f32)
        picked = jnp.zeros((8, BS), jnp.int32)
        for r in range(2):
            for k in range(3):
                picked = jnp.where(lane == 3 * r + k, columns[k, 0, side * (ROWS - 2) + r], picked)
        packed[side, SMALL + 16 : HALO] = picked.astype(f32)
    forward = [-spare[0]]
    for j in range(1, 4):
        forward.append(-product(mine[LOWER + j], forward[-1]))
    both = product(mine[PIVOT + 3], jnp.concatenate([forward[3], -spare[1]], axis=1))
    for j in (3, 2, 1, 0):
        if j < 3:
            both = product(mine[UPPER + j], both)
            both = product(mine[PIVOT + j], jnp.concatenate([forward[j] - both[:, :BS], -both[:, BS:]], axis=1))
        mine[inside_at(j)] = both[:, :BS]
        mine[inside_at(j) + 1] = both[:, BS:]
    odd = lax.axis_index("gy") % 2 == 1
    for at, value in enumerate((forward[3], both[:, :BS], both[:, BS:])):
        maps[at] = jnp.where(odd, value.T, value)
    for action in far:
        action.wait()
    sent = [
        pltpu.make_async_copy(packed.at[0], to_previous, out_sems.at[4]),
        pltpu.make_async_copy(packed.at[1], to_next, out_sems.at[5]),
        pltpu.make_async_copy(maps, maps_out, out_sems.at[0]),
        pltpu.make_async_copy(mine, mine_out, out_sems.at[1]),
        pltpu.make_async_copy(mine.at[pl.ds(0, FOR_PREVIOUS)], for_previous, out_sems.at[2]),
        pltpu.make_async_copy(mine.at[pl.ds(MINE - FOR_NEXT, FOR_NEXT)], for_next, out_sems.at[3]),
    ]
    for action in sent:
        action.start()
    for action in sent:
        action.wait()


def change_row(blocks, turned_block, source, picks):
    total = blocks[0] * source[pl.ds(picks[0], 1)]
    total += blocks[1] * source[pl.ds(picks[1], 1)]
    total += blocks[2] * source[pl.ds(picks[2], 1)]
    column = jnp.sum(total, axis=1, keepdims=True)
    if turned_block is None:
        return column
    return jnp.sum(turned_block * column, axis=0, keepdims=True)


def own_blocks(blocks, n):
    return [blocks[3 * n + k] for k in range(3)]


def halo_change(halo, r, source, picks):
    blocks = [halo[(3 * r + k) * BS : (3 * r + k + 1) * BS] for k in range(3)]
    return change_row(blocks, halo[TURNED + r * BS : TURNED + (r + 1) * BS], source, picks)


def picks_of(columns, n, base):
    return [jnp.clip(columns[k, 0, n] - base, 0, FEXT - 1) for k in range(3)]


def halo_picks(halo_columns, side, r, base):
    return [
        jnp.clip(halo_columns[side, 0, 3 * r + k].astype(jnp.int32) - base, 0, FEXT - 1) for k in range(3)]


def scattered(total, value, index, low_block):
    row8 = lax.broadcasted_iota(jnp.int32, (8, BS), 0)
    row128 = lax.broadcasted_iota(jnp.int32, (BS, BS), 0)
    block, within = (index >> 7) - low_block, index & 127
    value = jnp.where(row8 == block, value, 0.0)
    high = value.astype(jnp.bfloat16).astype(f32)
    parts = jnp.concatenate([high, value - high], axis=0).astype(jnp.bfloat16)
    hot = jnp.where(row128 == within, 1.0, 0.0).astype(jnp.bfloat16)
    return total + lax.dot_general(parts, hot, (((1,), (1,)), ((), ())), preferred_element_type=f32)


def interior_kernel(
    rhs, weights, aggregates, columns, fine, smoother, packed,
    turned_out, first_out, second_out, total_out,
    blocks, smooth, turned, first, second, residual, rows, indices, sems, small_sems, out_sems,
):
    gx = lax.axis_index("gx")
    low_block = lax.axis_index("gy") * 4 - 2
    eye = identity_mask()
    n_chunks = ROWS // CHUNK
    small = [
        pltpu.make_async_copy(rhs, rows.at[0], small_sems.at[0]),
        pltpu.make_async_copy(weights, rows.at[1], small_sems.at[1]),
        pltpu.make_async_copy(aggregates, indices, small_sems.at[2]),
    ]
    for action in small:
        action.start()

    def fetch(c):
        part = pl.ds(c * CHUNK, CHUNK)
        return pltpu.make_async_copy(smoother.at[part], smooth.at[part], sems.at[0, c])

    def block_copy(c):
        part = pl.ds(c * CHUNK * 3, CHUNK * 3)
        return pltpu.make_async_copy(fine.at[part], blocks.at[part], sems.at[1, c])

    def store(c):
        part = pl.ds(c * CHUNK, CHUNK)
        return pltpu.make_async_copy(turned.at[part], turned_out.at[part], out_sems.at[c])

    ahead = 2
    for c in range(ahead):
        fetch(c).start()
    for c in range(n_chunks):
        if c + ahead < n_chunks:
            fetch(c + ahead).start()
        block_copy(c).start()
    for action in small:
        action.wait()

    def first_row(n):
        block = smooth[n]
        turned[n] = block.T
        return column_to_row(jnp.sum(block * rows[0, n : n + 1], axis=1, keepdims=True), eye)

    base = gx * ROWS

    def picks(n):
        return [jnp.clip(columns[k, 0, n] - base, 0, ROWS - 1) for k in range(3)]

    def second_row(n):
        change = change_row(own_blocks(blocks, n), turned[n], first, picks(n))
        return 2.0 * first[n : n + 1] - change

    zero = jnp.zeros((1, BS), f32)
    for c in range(-ahead, n_chunks):
        new, old = c + ahead, c
        if new < n_chunks:
            fetch(new).wait()
        if old >= 0:
            block_copy(old).wait()
        found, done = [], []
        for r in range(CHUNK):
            if new < n_chunks:
                found.append(first_row(new * CHUNK + r))
            if old >= 0:
                n = old * CHUNK + r
                done.append(second_row(n) if 2 <= n < ROWS - 2 else zero)
        if found:
            first[new * CHUNK : new * CHUNK + CHUNK] = jnp.concatenate(found, axis=0)
            store(new).start()
        if done:
            second[old * CHUNK : old * CHUNK + CHUNK] = jnp.concatenate(done, axis=0)

    def residual_row(n, _):
        column = change_row(own_blocks(blocks, n), None, second, picks(n))
        residual[pl.ds(n, 1)] = column_to_row(column, eye)
        return 0

    lax.fori_loop(4, ROWS - 4, residual_row, 0, unroll=8)
    residual[...] = rows[1] * (rows[0] - residual[...])

    def scatter(n, total):
        return scattered(total, residual[pl.ds(n, 1)], indices[pl.ds(n, 1)], low_block)

    total_out[...] = lax.fori_loop(4, ROWS - 4, scatter, jnp.zeros((16, BS), f32), unroll=8)
    first_out[...] = first[...]
    second_out[...] = second[...]
    for c in range(n_chunks):
        store(c).wait()


def edges_kernel(
    rhs, weights, aggregates, columns, fine, turned_hbm, first, second, total_in, before, after,
    shared, first_field, second_own,
    blocks, turned, field, ends, indices, halo_columns, sems,
):
    gx = lax.axis_index("gx")
    low_block = lax.axis_index("gy") * 4 - 2
    eye = identity_mask()
    copies = []
    halo = (before, after)
    for side, source in enumerate(halo):
        top, near = side * (ROWS - 4), side * (ROWS - 8)
        for at, (src, dst) in enumerate((
            (source.at[pl.ds(SMALL + 16, 8)], halo_columns.at[side]),
            (fine.at[pl.ds(3 * top, 12)], blocks.at[side]),
            (turned_hbm.at[pl.ds(side * (ROWS - 2), 2)], turned.at[side]),
            (rhs.at[pl.ds(near, 8)], ends.at[side, 0]),
            (weights.at[pl.ds(near, 8)], ends.at[side, 1]),
            (aggregates.at[pl.ds(near, 8)], indices.at[side]),
        )):
            action = pltpu.make_async_copy(src, dst, sems.at[side, at])
            action.start()
            copies.append(action)
    base = gx * ROWS - 4
    first_field[4 : ROWS + 4] = first[...]
    field[4 : ROWS + 4] = second[...]
    field[0:2] = jnp.zeros((2, BS), f32)
    field[FEXT - 2 : FEXT] = jnp.zeros((2, BS), f32)
    for action in copies:
        action.wait()
    first_field[0:4] = before[SMALL : SMALL + 4]
    first_field[FEXT - 4 : FEXT] = after[SMALL : SMALL + 4]

    def edge_blocks(side, r):
        return [blocks[side, 3 * r + k] for k in range(3)]

    for side in range(2):
        for r in range(2):
            at = side * (ROWS + 2) + 2 + r
            change = halo_change(halo[side], r, first_field, halo_picks(halo_columns, side, r, base))
            field[at : at + 1] = 2.0 * first_field[at : at + 1] - change
            n = side * (ROWS - 2) + r
            change = change_row(
                edge_blocks(side, 2 * side + r), turned[side, r], first_field, picks_of(columns, n, base))
            field[n + 4 : n + 5] = 2.0 * first_field[n + 4 : n + 5] - change
    second_own[...] = field[4 : ROWS + 4]
    total = total_in[...]
    for side in range(2):
        for r in range(4):
            n, at = side * (ROWS - 4) + r, 4 * side + r
            column = change_row(edge_blocks(side, r), None, field, picks_of(columns, n, base))
            value = ends[side, 1, at : at + 1] * (ends[side, 0, at : at + 1] - column_to_row(column, eye))
            total = scattered(total, value, indices[side, at : at + 1], low_block)
    shared[0:8] = total[0:8] + total[8:16]
    shared[8:40] = jnp.zeros((32, BS), f32)
    shared[pl.ds(pl.multiple_of(8 + 8 * gx, 8), 8)] = jnp.concatenate(
        [field[4:8], field[FEXT - 8 : FEXT - 4]], axis=0)


def local_kernel(shared, mine, previous, following, out):
    eye = identity_mask()
    zero = jnp.zeros((1, BS), f32)
    own = [shared[j : j + 1] for j in range(8)]
    groups = (
        (previous, MINE - FOR_NEXT, [zero, zero, own[0], own[1]]),
        (mine, 0, own[2:6]),
        (following, 0, [own[6], own[7], zero, zero]),
    )
    inner = [[right[0]] for _, _, right in groups]
    for j in range(1, 4):
        for at, ((source, start, right), found) in enumerate(zip(groups, inner)):
            if at == 0 and j < 3:
                found.append(right[j])
            else:
                found.append(right[j] - times_row(source[LOWER + j - start], found[-1], eye))
    solved = [[None] * 4 for _ in groups]
    for j in (3, 2, 1, 0):
        held = []
        for (source, start, _), found, x in zip(groups, inner, solved):
            held.append(
                found[j] if j == 3 else found[j] - times_row(source[UPPER + j - start], x[j + 1], eye))
        for (source, start, _), value, x in zip(groups, held, solved):
            x[j] = times_row(source[PIVOT + j - start], value, eye)
    tiles = []
    for found, x in zip(inner, solved):
        tiles += x + [found[3], zero, zero, zero]
    tile = jnp.concatenate(tiles, axis=0)
    for peer in range(GROUPS):
        out[peer] = tile


def correct_kernel(
    parts_hbm, shared, first_field, second_own, weights, aggregates, columns, maps, mine, previous, following,
    fine, turned_hbm, before_hbm, after_hbm,
    field_out, coarse_out,
    parts, chain, inside, blocks, turned, halo, sums, entering, leaving, window, field, next_field, halo_columns,
    weight_rows, indices, sems, chain_sems, block_sems,
):
    gx = lax.axis_index("gx")
    gy = lax.axis_index("gy")
    eye = identity_mask()
    step = 8
    chain_copies = {}
    arrived = pltpu.make_async_copy(parts_hbm, parts, sems.at[4])
    arrived.start()
    n_steps = GROUPS // step
    for kind, c in [(k, c) for c in range(n_steps) for k in (0, 1)] + [(2, c) for c in reversed(range(n_steps))]:
        action = pltpu.make_async_copy(
            maps.at[pl.ds(c * step, step), kind], chain.at[kind, pl.ds(c * step, step)], chain_sems.at[kind, c])
        action.start()
        chain_copies[kind, c] = action
    copies = [
        pltpu.make_async_copy(previous.at[pl.ds(FOR_NEXT - 4, 4)], inside.at[pl.ds(0, 4)], sems.at[5]),
        pltpu.make_async_copy(mine.at[pl.ds(0, 4)], inside.at[pl.ds(4, 4)], sems.at[6]),
        pltpu.make_async_copy(mine.at[pl.ds(MINE - 4, 4)], inside.at[pl.ds(8, 4)], sems.at[11]),
        pltpu.make_async_copy(following.at[pl.ds(0, 4)], inside.at[pl.ds(12, 4)], sems.at[7]),
        pltpu.make_async_copy(before_hbm.at[pl.ds(SMALL + 16, 8)], halo_columns.at[0], sems.at[0]),
        pltpu.make_async_copy(after_hbm.at[pl.ds(SMALL + 16, 8)], halo_columns.at[1], sems.at[1]),
        pltpu.make_async_copy(weights, weight_rows, sems.at[2]),
        pltpu.make_async_copy(aggregates, indices, sems.at[3]),
        pltpu.make_async_copy(before_hbm, halo.at[0], sems.at[8]),
        pltpu.make_async_copy(after_hbm, halo.at[1], sems.at[9]),
    ]
    whole = [pltpu.make_async_copy(turned_hbm, turned, sems.at[10])]
    for c in range(4):
        rows = pl.ds(c * (ROWS * 3 // 4), ROWS * 3 // 4)
        whole.append(pltpu.make_async_copy(fine.at[rows], blocks.at[rows], block_sems.at[c]))
    for action in copies + whole:
        action.start()
    before, after = halo.at[0], halo.at[1]
    arrived.wait()

    for d in range(GROUPS):
        total = parts[d, 8:16]
        if d + 1 < GROUPS:
            total += parts[d + 1, 0:8]
        if d > 0:
            total += parts[d - 1, 16:24]
        sums[d + 1] = total
    sums[0] = jnp.zeros((8, BS), f32)
    sums[GROUPS + 1] = jnp.zeros((8, BS), f32)

    entering[0:8] = jnp.zeros((8, BS), f32)
    value = jnp.zeros((1, BS), f32)
    heights = []
    for d in range(GROUPS):
        if d % step == 0:
            for kind in (0, 1):
                chain_copies[kind, d // step].wait()
        own, local = sums[d + 1, 4:5], sums[d + 1, 0:1]
        if d % 2 == 0:
            height = jnp.sum(chain[1, d] * value + jnp.where(eye, local, 0.0), axis=1, keepdims=True)
            value = jnp.sum(chain[0, d] * value + jnp.where(eye, own, 0.0), axis=1, keepdims=True)
            entering[d + 1 : d + 2] = column_to_row(value, eye)
        else:
            height = jnp.sum(chain[1, d] * value, axis=0, keepdims=True) + local
            value = jnp.sum(chain[0, d] * value, axis=0, keepdims=True) + own
            entering[d + 1 : d + 2] = value
        heights.append(column_to_row(height, eye) if d % 2 == 0 else height)
    leaving[GROUPS : GROUPS + 8] = jnp.zeros((8, BS), f32)
    value = None
    for d in reversed(range(GROUPS)):
        if d % step == step - 1:
            chain_copies[2, d // step].wait()
        if d == GROUPS - 1:
            value = heights[d]
        elif d % 2 == 0:
            value = jnp.sum(chain[2, d] * value + jnp.where(eye, heights[d], 0.0), axis=1, keepdims=True)
        else:
            value = jnp.sum(chain[2, d] * value, axis=0, keepdims=True) + heights[d]
        leaving[d : d + 1] = column_to_row(value, eye) if d % 2 == 0 else value

    for action in copies[:4]:
        action.wait()
    for j in range(8):
        offset, block = ((-1, j + 2), (0, j - 2), (1, j - 6))[(j + 2) // 4]
        group = gy + offset
        enter = entering[pl.ds(jnp.maximum(group, 0), 1)]
        leave = leaving[pl.ds(jnp.minimum(group + 1, GROUPS), 1)]
        total = inside[2 * j] * enter + inside[2 * j + 1] * leave
        window[j : j + 1] = column_to_row(jnp.sum(total, axis=1, keepdims=True), eye) + sums[
            group + 1, block : block + 1]
    coarse_out[...] = window[2:6]

    for action in copies[4:]:
        action.wait()
    low_block = gy * 4 - 2
    field[4 : ROWS + 4] = second_own[...]
    left = pl.multiple_of(8 + 8 * jnp.maximum(gx - 1, 0), 8)
    right = pl.multiple_of(8 + 8 * jnp.minimum(gx + 1, 3), 8)
    field[0:4] = shared[pl.ds(left, 8)][4:8]
    field[FEXT - 4 : FEXT] = shared[pl.ds(right, 8)][0:4]

    def interpolate(index, weight):
        block, within = (index >> 7) - low_block, index & 127
        total = jnp.zeros(index.shape, f32)
        for j in range(8):
            source = jnp.broadcast_to(window[j : j + 1], index.shape)
            total = jnp.where(block == j, jnp.take_along_axis(source, within, axis=1), total)
        return weight * total

    for at in range(ROWS // 8):
        rows = pl.ds(8 * at, 8)
        field[pl.ds(8 * at + 4, 8)] += interpolate(indices[rows], weight_rows[rows])
    for top, source in ((0, before), (FEXT - 4, after)):
        index = source[SMALL + 8 : SMALL + 16].astype(jnp.int32)
        weight = jnp.concatenate([source[SMALL + 4 : SMALL + 8], jnp.zeros((4, BS), f32)], axis=0)
        field[top : top + 4] += interpolate(index, weight)[0:4]

    base = gx * ROWS - 4
    next_field[0:2] = jnp.zeros((2, BS), f32)
    next_field[FEXT - 2 : FEXT] = jnp.zeros((2, BS), f32)
    whole[0].wait()

    def third(n, _):
        change = change_row(own_blocks(blocks, n), turned[n], field, picks_of(columns, n, base))
        rows = pl.ds(n + 4, 1)
        next_field[rows] = field[rows] + first_field[rows] - change
        return 0

    for c in range(4):
        whole[1 + c].wait()
        lax.fori_loop(c * ROWS // 4, (c + 1) * ROWS // 4, third, 0, unroll=8)
    for side, source in ((0, before), (1, after)):
        for r in range(2):
            at = side * (ROWS + 2) + 2 + r
            change = halo_change(source, r, field, halo_picks(halo_columns, side, r, base))
            next_field[at : at + 1] = field[at : at + 1] + first_field[at : at + 1] - change

    def fourth(n, _):
        change = change_row(own_blocks(blocks, n), turned[n], next_field, picks_of(columns, n, base))
        rows = pl.ds(n + 4, 1)
        field_out[pl.ds(n, 1)] = next_field[rows] + first_field[rows] - change
        return 0

    lax.fori_loop(0, ROWS, fourth, 0, unroll=8)


def per_device(
    rhs, fine_blocks, smoother, columns, aggregates, weights, coarse_lower, coarse_upper, coarse_pivot
):
    rhs, aggregates, weights, columns, smoother = rhs[0], aggregates[0], weights[0], columns.transpose(2, 0, 1), smoother[0]
    fine = fine_blocks.reshape(ROWS * 3, BS, BS)
    dma = pltpu.SemaphoreType.DMA

    maps, mine, for_previous, for_next, to_previous, to_next = pl.pallas_call(
        prepare_kernel,
        name="prepare",
        out_shape=(
            shape(3, BS, BS), shape(MINE, BS, BS), shape(FOR_PREVIOUS, BS, BS), shape(FOR_NEXT, BS, BS),
            shape(HALO, BS), shape(HALO, BS)),
        in_specs=[HBM] * 6 + [SMEM] + [HBM] * 2,
        out_specs=(HBM,) * 6,
        scratch_shapes=[
            pltpu.VMEM((3, BS, BS), f32), pltpu.VMEM((MINE, BS, BS), f32), pltpu.VMEM((2, BS, BS), f32),
            pltpu.VMEM((2, HALO, BS), f32), pltpu.VMEM((2, 4, BS, BS), f32), pltpu.VMEM((2, 2, 8, BS), f32),
            pltpu.VMEM((2, 8, BS), jnp.int32), dma((5,)), dma((2, 5)), dma((6,)),
        ],
        compiler_params=grant(58),
    )(
        coarse_lower, coarse_upper, coarse_pivot, rhs, weights, aggregates, columns,
        fine_blocks.reshape(ROWS * 3 * BS, BS), smoother,
    )
    gathered = lax.all_gather(maps, "gy", axis=0)

    before = lax.ppermute(to_next, "gx", [(i, i + 1) for i in range(3)])
    after = lax.ppermute(to_previous, "gx", [(i + 1, i) for i in range(3)])

    turned, first, second, total = pl.pallas_call(
        interior_kernel,
        name="interior",
        out_shape=(shape(ROWS, BS, BS), shape(ROWS, BS), shape(ROWS, BS), shape(16, BS)),
        in_specs=[HBM] * 3 + [SMEM] + [HBM] * 3,
        out_specs=(HBM, VMEM, VMEM, VMEM),
        scratch_shapes=[
            pltpu.VMEM((ROWS * 3, BS, BS), f32), pltpu.VMEM((ROWS, BS, BS), f32), pltpu.VMEM((ROWS, BS, BS), f32),
            pltpu.VMEM((ROWS, BS), f32), pltpu.VMEM((ROWS, BS), f32), pltpu.VMEM((ROWS, BS), f32),
            pltpu.VMEM((2, ROWS, BS), f32), pltpu.VMEM((ROWS, BS), jnp.int32),
            dma((2, ROWS // CHUNK)), dma((3,)), dma((ROWS // CHUNK,)),
        ],
        compiler_params=grant(58),
    )(rhs, weights, aggregates, columns, fine, smoother, to_next)

    shared, first_field, second_own = pl.pallas_call(
        edges_kernel,
        name="edges",
        out_shape=(shape(40, BS), shape(FEXT, BS), shape(ROWS, BS)),
        in_specs=[HBM] * 3 + [SMEM] + [HBM] * 2 + [VMEM] * 5,
        out_specs=(VMEM, VMEM, VMEM),
        scratch_shapes=[
            pltpu.VMEM((2, 12, BS, BS), f32), pltpu.VMEM((2, 2, BS, BS), f32),
            pltpu.VMEM((FEXT, BS), f32), pltpu.VMEM((2, 2, 8, BS), f32), pltpu.VMEM((2, 8, BS), jnp.int32),
            pltpu.SMEM((2, 8, BS), f32), dma((2, 6)),
        ],
        compiler_params=grant(54),
    )(rhs, weights, aggregates, columns, fine, turned, first, second, total, before, after)
    previous = lax.ppermute(for_next, "gy", [(i, i + 1) for i in range(GROUPS - 1)])
    following = lax.ppermute(for_previous, "gy", [(i + 1, i) for i in range(GROUPS - 1)])
    for bit in (1, 2):
        shared = shared + lax.ppermute(shared, "gx", [(i, i ^ bit) for i in range(4)])

    spread = pl.pallas_call(
        local_kernel,
        name="local_solutions",
        out_shape=shape(GROUPS, 24, BS),
        in_specs=[VMEM] * 4,
        out_specs=VMEM,
        compiler_params=grant(40),
    )(shared, mine, previous, following)
    parts = lax.all_to_all(spread, "gy", 0, 0)

    field, coarse = pl.pallas_call(
        correct_kernel,
        name="correct",
        out_shape=(shape(ROWS, BS), shape(4, BS)),
        in_specs=[HBM] + [VMEM] * 3 + [HBM] * 2 + [SMEM] + [HBM] * 8,
        out_specs=(VMEM, VMEM),
        scratch_shapes=[
            pltpu.VMEM((GROUPS, 24, BS), f32), pltpu.VMEM((3, GROUPS, BS, BS), f32), pltpu.VMEM((16, BS, BS), f32),
            pltpu.VMEM((ROWS * 3, BS, BS), f32), pltpu.VMEM((ROWS, BS, BS), f32), pltpu.VMEM((2, HALO, BS), f32),
            pltpu.VMEM((GROUPS + 2, 8, BS), f32),
            pltpu.VMEM((GROUPS + 8, BS), f32), pltpu.VMEM((GROUPS + 8, BS), f32), pltpu.VMEM((8, BS), f32),
            pltpu.VMEM((FEXT, BS), f32), pltpu.VMEM((FEXT, BS), f32), pltpu.SMEM((2, 8, BS), f32),
            pltpu.VMEM((ROWS, BS), f32), pltpu.VMEM((ROWS, BS), jnp.int32), dma((12,)), dma((3, 4)), dma((4,)),
        ],
        compiler_params=grant(58),
    )(
        parts, shared, first_field, second_own, weights, aggregates, columns, gathered, mine, previous, following,
        fine, turned, before, after,
    )
    return (field[None], coarse)


def solution(mesh):
    return jax.shard_map(
        per_device,
        mesh=mesh,
        in_specs=(
            P("gy", "gx", None),
            P("gy", "gx", None, None, None),
            P("gy", "gx", None, None),
            P("gy", "gx", None),
            P("gy", "gx", None),
            P("gy", "gx", None),
            P("gy", None, None),
            P("gy", None, None),
            P("gy", None, None),
        ),
        out_specs=(P("gy", "gx", None), P("gy", None)),
        check_vma=False,
    )
```
